128 devices in a mesh: row: 16 (over z, x), col: 8 (over y, core).
Axes of the slice: x: 4, y: 4, z: 4, core: 2. Of those that a mesh axis runs over, the one named last changes fastest.
Arguments:
- alignment_tensor: bfloat16 [1024, 32768], P('row', 'col'), may hold values from -20 to 20
- supplement_align_cover: int32 [1024, 512], P('row', 'col'), may hold values from 0 to 1, as said below
- couple_tensor: float32 [512, 512, 128], P('row', 'col'), may hold values from -6 to 6
- couple_cover_grid: int32 [512, 512], P('row', 'col'), may hold values 0 or 1
- amino_strand_label: int32 [512], replicated, may hold values from 0 to 3, never falling along the last dimension, each value on 1 to 256 neighbouring positions
- focus_scaling_vector: float32 [64], replicated, may hold values from 0.5 to 12
- focus_asking_factor: bfloat16 [64, 64], replicated, may hold values from -0.75 to 0.75
- focus_lookup_factor: bfloat16 [64, 8], replicated, may hold values from -0.75 to 0.75
- focus_content_factor: bfloat16 [64, 8], replicated, may hold values from -0.75 to 0.75
- focus_sigmoid_factor: bfloat16 [64, 64], replicated, may hold values from -0.75 to 0.75
- focus_final_factor: bfloat16 [64, 64], replicated, may hold values from -0.75 to 0.75
- dyadic_scaling_vector: float32 [64], replicated, may hold values from 0.5 to 1.5
- dyadic_first_factor: bfloat16 [64, 32], replicated, may hold values from -0.75 to 0.75
- dyadic_second_factor: bfloat16 [64, 32], replicated, may hold values from -0.75 to 0.75
- dyadic_final_factor: bfloat16 [1024, 128], replicated, may hold values from -1 to 1
- strand_couple_table: float32 [2, 128], replicated, may hold values from -4 to 4
- trio_source_scaling: float32 [128], replicated, may hold values from 0.5 to 1.5
- trio_mapping_factors: bfloat16 [128, 512], replicated, may hold values from -0.5 to 0.5
- trio_sigmoid_factor: bfloat16 [128, 128], replicated, may hold values from -0.5 to 0.5
- trio_middle_scaling: float32 [128], replicated, may hold values from 0.5 to 1.5
- trio_final_factor: bfloat16 [128, 128], replicated, may hold values from -0.5 to 0.5
Outputs:
- refreshed_supplement_align: bfloat16 [1024, 32768], P('row', 'col')
- refreshed_couple_tensor: float32 [512, 512, 128], P('row', 'col')
The draws below stay inside these ranges and needn't reach their ends.
Inputs may be any that keep to these rules, and one draw needn't show every extreme that they name: `supplement_align_cover`: a trailing run of residues is 0 in every sequence.
All inputs are finite; a program needn't handle non-finite values. No bound on the sum of `couple_cover_grid` on one device may be relied on, other than what follows from the above.
Results may differ from the reference program's by a relative error of at most 0.0072.
Values may be sent and summed in bfloat16 or wider, within the bound.
No kernel may reach another device: no remote copies, remote signals or barrier semaphores. Data moves between devices by JAX's collectives and lax.ppermute only.
A program may use at most 128 MiB of HBM per device.

```python
import math
import jax
import jax.numpy as jnp
import numpy as np
from jax import lax

ALIGN_FEATURES = 64
C_Z = 128
PRODUCT_FEATURES = 32
C_TRI = 128
FOCUS_BRANCHES = 8
BRANCH_FEATURES = 8
RES_ROW = 32
SUPPLEMENT_ALIGNS = 1024
AMINO_TOTAL = 512
N_ROW = 16


def draw_alignment_tensor(key, part):
    key = jax.random.fold_in(key, 11)
    lookup_shared, random_seed_draw = jax.random.split(key, 2)
    shared_content = jax.random.normal(lookup_shared, (AMINO_TOTAL, ALIGN_FEATURES), jnp.float32)
    random_jitter = 0.8 * jax.random.normal(random_seed_draw, (SUPPLEMENT_ALIGNS, AMINO_TOTAL, ALIGN_FEATURES), jnp.float32)
    return (shared_content[None] + random_jitter).reshape(SUPPLEMENT_ALIGNS, AMINO_TOTAL * ALIGN_FEATURES).astype(jnp.bfloat16)


def draw_supplement_align_cover(key, part):
    key = jax.random.fold_in(key, 12)
    key_pad, key_live = jax.random.split(key)
    padding = jax.random.randint(key_pad, (), 1, AMINO_TOTAL // 8 + 1)
    live = jax.random.randint(key_live, (SUPPLEMENT_ALIGNS, AMINO_TOTAL), 0, 20) < 17
    position = jnp.arange(AMINO_TOTAL)
    kept = live & (position < AMINO_TOTAL - padding)[None, :]
    return jnp.where(kept, 1, 0).astype(jnp.int32)


def draw_focus_scaling_vector(key, part):
    key = jax.random.fold_in(key, 13)
    return jax.random.uniform(key, (ALIGN_FEATURES,), jnp.float32, 0.7, 1.3)


def plant(entries, key, least, top_value):
    longest = entries.shape.index(max(entries.shape))
    spots = []
    for shift in (0, 1):
        where = [jax.random.randint(jax.random.fold_in(key, axis), (), 0, length) for axis, length in enumerate(entries.shape)]
        where[longest] = (where[longest] + shift) % entries.shape[longest]
        spots.append(tuple(where))
    return entries.at[spots[0]].set(least).at[spots[1]].set(top_value)


def block_levels(stream_key, shape, cuts, smallest, largest):
    factor_of, own = 1.0, jax.random.fold_in(stream_key, 6)
    for dim, shards_of in cuts:
        heights = jnp.exp(jax.random.uniform(jax.random.fold_in(own, dim), (shards_of,), jnp.float32, smallest / len(cuts), largest / len(cuts)))
        factor_of = factor_of * jnp.repeat(heights, shape[dim] // shards_of).reshape([-1 if axis == dim else 1 for axis in range(len(shape))])
    return factor_of


def split_up(count, total, limit, slope):
    loads = [(1 << 20) // math.isqrt(grade ** slope) + 1 for grade in range(2, count + 1)]
    spare, given = total - limit - (count - 1), [1] * (count - 1)
    while spare > 0:
        candidates = [i for i in range(count - 1) if given[i] < limit]
        mass, remaining = sum([loads[i] for i in candidates]), spare
        for i in candidates:
            extra = min(limit - given[i], max(1, remaining * loads[i] // mass), spare)
            given[i] = given[i] + extra
            spare = spare - extra
    return np.array([limit] + given)


def ragged_sizes(key, number_of, total, limit, lean):
    if number_of == 2:
        one = jax.random.randint(key, (), max(1, total - limit), min(limit, total - 1) + 1)
        return jnp.stack([one, total - one])
    lengths = jnp.asarray(split_up(number_of, total, limit, lean), jnp.int32)
    pairs = (number_of - 1) // 2
    giver, taker = lengths[1:1 + 2 * pairs:2], lengths[2:2 + 2 * pairs:2]
    room = jnp.minimum(giver - 1, limit - taker)
    shifted = jax.random.randint(jax.random.fold_in(key, 1), (pairs,), 0, 1 << 20) % (room + 1)
    lengths = lengths.at[1:1 + 2 * pairs:2].set(giver - shifted).at[2:2 + 2 * pairs:2].set(taker + shifted)
    return lengths[jax.random.permutation(jax.random.fold_in(key, 2), number_of)]


def gaussian(own_key, dims, deviation, most, pieces=(), held_as=jnp.bfloat16):
    level = block_levels(own_key, dims, pieces, -0.22, 0.18) if pieces else 1.0
    result = jax.random.normal(own_key, dims, jnp.float32) * deviation * level
    return jnp.minimum(jnp.maximum(result, -most), most).astype(held_as)


def setup_inputs(seed: int = 0) -> dict:
    seeds = jax.random.split(jax.random.key(seed), 22)
    return {
        "alignment_tensor": draw_alignment_tensor(jax.random.fold_in(seeds[21], 71), 0),
        "supplement_align_cover": draw_supplement_align_cover(jax.random.fold_in(seeds[21], 71), 0),
        "couple_tensor": gaussian(seeds[2], (AMINO_TOTAL, AMINO_TOTAL, C_Z), 1.0, 6.0, ((0, 16), (1, 8)), jnp.float32),
        "couple_cover_grid": plant((jax.random.randint(seeds[3], (AMINO_TOTAL, AMINO_TOTAL), 0, 10) < 9).astype(jnp.int32), jax.random.fold_in(seeds[3], 1), 0, 1),
        "amino_strand_label": jnp.searchsorted(jnp.cumsum(ragged_sizes(seeds[4], 4, AMINO_TOTAL, AMINO_TOTAL // 2, 0)), jnp.arange(AMINO_TOTAL), side="right").astype(jnp.int32),
        "focus_scaling_vector": draw_focus_scaling_vector(jax.random.fold_in(seeds[21], 71), 0),
        "focus_asking_factor": gaussian(seeds[6], (ALIGN_FEATURES, FOCUS_BRANCHES * BRANCH_FEATURES), ALIGN_FEATURES ** -0.5, 0.75),
        "focus_lookup_factor": gaussian(seeds[7], (ALIGN_FEATURES, BRANCH_FEATURES), ALIGN_FEATURES ** -0.5, 0.75),
        "focus_content_factor": gaussian(seeds[8], (ALIGN_FEATURES, BRANCH_FEATURES), ALIGN_FEATURES ** -0.5, 0.75),
        "focus_sigmoid_factor": gaussian(seeds[9], (ALIGN_FEATURES, FOCUS_BRANCHES * BRANCH_FEATURES), ALIGN_FEATURES ** -0.5, 0.75),
        "focus_final_factor": gaussian(seeds[10], (FOCUS_BRANCHES * BRANCH_FEATURES, ALIGN_FEATURES), (FOCUS_BRANCHES * BRANCH_FEATURES) ** -0.5, 0.75),
        "dyadic_scaling_vector": jnp.clip(1.0 + 0.1 * jax.random.normal(seeds[11], (ALIGN_FEATURES,), jnp.float32), 0.5, 1.5),
        "dyadic_first_factor": gaussian(seeds[12], (ALIGN_FEATURES, PRODUCT_FEATURES), ALIGN_FEATURES ** -0.5, 0.75),
        "dyadic_second_factor": gaussian(seeds[13], (ALIGN_FEATURES, PRODUCT_FEATURES), ALIGN_FEATURES ** -0.5, 0.75),
        "dyadic_final_factor": gaussian(seeds[14], (PRODUCT_FEATURES * PRODUCT_FEATURES, C_Z), PRODUCT_FEATURES ** -0.5, 1.0),
        "strand_couple_table": gaussian(seeds[15], (2, C_Z), 1.0, 4.0, (), jnp.float32),
        "trio_source_scaling": jnp.clip(1.0 + 0.1 * jax.random.normal(seeds[16], (C_Z,), jnp.float32), 0.5, 1.5),
        "trio_mapping_factors": gaussian(seeds[17], (C_Z, 4 * C_TRI), C_Z ** -0.5, 0.5),
        "trio_sigmoid_factor": gaussian(seeds[18], (C_Z, C_Z), C_Z ** -0.5, 0.5),
        "trio_middle_scaling": jnp.clip(1.0 + 0.1 * jax.random.normal(seeds[19], (C_TRI,), jnp.float32), 0.5, 1.5),
        "trio_final_factor": gaussian(seeds[20], (C_TRI, C_Z), C_TRI ** -0.5, 0.5),
    }


def standardize_features(x, gain):
    mean = lax.optimization_barrier(jnp.mean(x, -1, keepdims=True))
    centred = x - mean
    var = lax.optimization_barrier(jnp.mean(centred * centred, -1, keepdims=True))
    return centred * lax.rsqrt(var + 1e-05) * gain

def reference(alignment_tensor, supplement_align_cover, couple_tensor, couple_cover_grid, amino_strand_label, focus_scaling_vector, focus_asking_factor, focus_lookup_factor, focus_content_factor, focus_sigmoid_factor, focus_final_factor, dyadic_scaling_vector, dyadic_first_factor, dyadic_second_factor, dyadic_final_factor, strand_couple_table, trio_source_scaling, trio_mapping_factors, trio_sigmoid_factor, trio_middle_scaling, trio_final_factor):
    hi = lax.Precision.HIGHEST
    alignment_cube = alignment_tensor.reshape(SUPPLEMENT_ALIGNS, AMINO_TOTAL, ALIGN_FEATURES).astype(jnp.float32)
    covered_contents = supplement_align_cover.astype(jnp.float32)
    focus_source = standardize_features(alignment_cube, focus_scaling_vector).astype(jnp.bfloat16)
    counts = jnp.maximum(lax.optimization_barrier(jnp.sum(covered_contents, 0)), 1.0)
    query_mean = (lax.optimization_barrier(jnp.sum(covered_contents[:, :, None] * focus_source.astype(jnp.float32), 0)) / counts[:, None]).astype(jnp.bfloat16)
    query = (jnp.dot(query_mean, focus_asking_factor, preferred_element_type=jnp.float32) * BRANCH_FEATURES ** (-0.5)).reshape(AMINO_TOTAL, FOCUS_BRANCHES, BRANCH_FEATURES)
    flattened_source = focus_source.reshape(SUPPLEMENT_ALIGNS * AMINO_TOTAL, ALIGN_FEATURES)
    keys = jnp.dot(flattened_source, focus_lookup_factor, preferred_element_type=jnp.float32).reshape(SUPPLEMENT_ALIGNS, AMINO_TOTAL, BRANCH_FEATURES)
    values = jnp.dot(flattened_source, focus_content_factor, preferred_element_type=jnp.float32).reshape(SUPPLEMENT_ALIGNS, AMINO_TOTAL, BRANCH_FEATURES)
    logits = jnp.einsum('rhd,srd->rhs', query, keys, precision=hi)
    logits = logits + jnp.where(covered_contents.T[:, None, :] > 0, 0.0, -1000000000.0).astype(jnp.float32)
    weights = jax.nn.softmax(logits, -1)
    mixed = jnp.einsum('rhs,srd->rhd', weights, values, precision=hi).reshape(AMINO_TOTAL, FOCUS_BRANCHES * BRANCH_FEATURES)
    gates = jax.nn.sigmoid(jnp.dot(flattened_source, focus_sigmoid_factor, preferred_element_type=jnp.float32)).reshape(SUPPLEMENT_ALIGNS, AMINO_TOTAL, FOCUS_BRANCHES * BRANCH_FEATURES)
    sigmoid_scaled_result = (gates * mixed[None]).astype(jnp.bfloat16).reshape(SUPPLEMENT_ALIGNS * AMINO_TOTAL, FOCUS_BRANCHES * BRANCH_FEATURES)
    refreshed_supplement_align = (alignment_cube + jnp.dot(sigmoid_scaled_result, focus_final_factor, preferred_element_type=jnp.float32).reshape(SUPPLEMENT_ALIGNS, AMINO_TOTAL, ALIGN_FEATURES)).astype(jnp.bfloat16).reshape(SUPPLEMENT_ALIGNS, AMINO_TOTAL * ALIGN_FEATURES)
    product_source = standardize_features(alignment_cube, dyadic_scaling_vector).astype(jnp.bfloat16).reshape(SUPPLEMENT_ALIGNS * AMINO_TOTAL, ALIGN_FEATURES)
    left = (jnp.dot(product_source, dyadic_first_factor, preferred_element_type=jnp.float32).reshape(SUPPLEMENT_ALIGNS, AMINO_TOTAL, PRODUCT_FEATURES) * covered_contents[:, :, None]).astype(jnp.bfloat16)
    right = (jnp.dot(product_source, dyadic_second_factor, preferred_element_type=jnp.float32).reshape(SUPPLEMENT_ALIGNS, AMINO_TOTAL, PRODUCT_FEATURES) * covered_contents[:, :, None]).astype(jnp.bfloat16)
    left_blocks = left.reshape(SUPPLEMENT_ALIGNS, N_ROW, RES_ROW * PRODUCT_FEATURES).transpose(1, 0, 2)
    mask_blocks = covered_contents.reshape(SUPPLEMENT_ALIGNS, N_ROW, RES_ROW).transpose(1, 0, 2)
    right_flat = right.reshape(SUPPLEMENT_ALIGNS, AMINO_TOTAL * PRODUCT_FEATURES)

    def opm_block(block):
        left_block, mask_block = block
        outer = lax.dot_general(left_block, right_flat, (((0,), (0,)), ((), ())), preferred_element_type=jnp.float32)
        outer = outer.reshape(RES_ROW, PRODUCT_FEATURES, AMINO_TOTAL, PRODUCT_FEATURES).transpose(0, 2, 1, 3).astype(jnp.bfloat16).reshape(RES_ROW * AMINO_TOTAL, PRODUCT_FEATURES * PRODUCT_FEATURES)
        projected = jnp.dot(outer, dyadic_final_factor, preferred_element_type=jnp.float32).reshape(RES_ROW, AMINO_TOTAL, C_Z)
        pair_count = lax.dot_general(mask_block, covered_contents, (((0,), (0,)), ((), ())), precision=hi)
        return projected / jnp.maximum(pair_count, 1.0)[:, :, None]
    update = lax.map(opm_block, (left_blocks, mask_blocks)).reshape(AMINO_TOTAL, AMINO_TOTAL, C_Z)
    same = amino_strand_label[:, None] == amino_strand_label[None, :]
    pair_mid = couple_tensor + update + jnp.where(same[:, :, None], strand_couple_table[1], strand_couple_table[0])
    tri_in = standardize_features(pair_mid, trio_source_scaling).astype(jnp.bfloat16).reshape(AMINO_TOTAL * AMINO_TOTAL, C_Z)
    proj = jnp.dot(tri_in, trio_mapping_factors, preferred_element_type=jnp.float32).reshape(AMINO_TOTAL, AMINO_TOTAL, 4 * C_TRI)
    pmask = couple_cover_grid.astype(jnp.float32)[:, :, None]
    tri_left = (pmask * jax.nn.sigmoid(proj[..., :C_TRI]) * proj[..., C_TRI:2 * C_TRI]).astype(jnp.bfloat16)
    tri_right = (pmask * jax.nn.sigmoid(proj[..., 2 * C_TRI:3 * C_TRI]) * proj[..., 3 * C_TRI:]).astype(jnp.bfloat16)
    product = jnp.einsum('ikc,jkc->ijc', tri_left.astype(jnp.float32), tri_right.astype(jnp.float32), precision=hi)
    centered = standardize_features(product, trio_middle_scaling).astype(jnp.bfloat16).reshape(AMINO_TOTAL * AMINO_TOTAL, C_TRI)
    out_gate = jax.nn.sigmoid(jnp.dot(tri_in, trio_sigmoid_factor, preferred_element_type=jnp.float32))
    refreshed_couple_tensor = pair_mid + (out_gate * jnp.dot(centered, trio_final_factor, preferred_element_type=jnp.float32)).reshape(AMINO_TOTAL, AMINO_TOTAL, C_Z)
    return (refreshed_supplement_align, refreshed_couple_tensor)
```

```python
import jax
import jax.numpy as jnp
from jax import lax
from jax.experimental import pallas as pl
from jax.experimental.pallas import tpu as pltpu
from jax.sharding import PartitionSpec as P

LANES = 128
HALF = 64
VMEM_LIMIT = 50 * 1024 * 1024


def standardize_features(x, gain):
    mean = jnp.mean(x, -1, keepdims=True)
    centred = x - mean
    var = jnp.mean(centred * centred, -1, keepdims=True)
    return centred * lax.rsqrt(var + 1e-05) * gain


def lane_index(shape):
    return lax.broadcasted_iota(jnp.int32, shape, len(shape) - 1)


def pair_kernel(
    left_a_ref,
    left_b_ref,
    left_mask_ref,
    right_ref,
    final_ref,
    couple_ref,
    cover_ref,
    same_ref,
    table_ref,
    gain_ref,
    mapping_ref,
    mid_ref,
    source_ref,
    sent_ref,
    outer_ref,
    count_ref,
    sides_ref,
):
    step = pl.program_id(0)
    steps = pl.num_programs(0)
    rows = 4
    low = lane_index((LANES, LANES)) < HALF

    @pl.when(step == 0)
    def _():
        both = lax.dot_general(
            left_mask_ref[...],
            right_ref[:, 2048:2176],
            (((0,), (0,)), ((), ())),
            preferred_element_type=jnp.float32,
        )
        both = jnp.maximum(both[:32], 1.0)
        count_ref[...] = jnp.where(lane_index((16, LANES)) < HALF, both[:16], both[16:])

    left = jnp.concatenate([left_a_ref[...], left_b_ref[...]], axis=1).T
    for n in range(8):
        outer_ref[:, n * 256 : (n + 1) * 256] = jnp.dot(
            left, right_ref[:, n * 256 : (n + 1) * 256], preferred_element_type=jnp.float32
        ).astype(jnp.bfloat16)

    sources = []
    for p in range(rows):
        halves = []
        for top in (p * 32, 128 + p * 32):
            halves.append(
                jnp.concatenate(
                    [outer_ref[top : top + 32, d * LANES : (d + 1) * LANES] for d in range(16)],
                    axis=0,
                )
            )
        update = jnp.dot(
            final_ref[...],
            jnp.concatenate(halves, axis=1),
            preferred_element_type=jnp.float32,
        )
        a0, a1 = update[:LANES, :LANES], update[LANES:, :LANES]
        b0, b1 = update[:LANES, LANES:], update[LANES:, LANES:]
        update = jnp.where(low, a0, b1) + pltpu.roll(jnp.where(low, b0, a1), HALF, 1)
        here = pl.ds(step * rows + p, 1)
        update = update / count_ref[here, :]
        update = update + jnp.where(same_ref[here, :] > 0, table_ref[:, 1:2], table_ref[:, 0:1])
        mid = couple_ref[:, p].reshape(LANES, LANES) + update.T
        mid_ref[:, p] = mid.reshape(2, HALF, LANES)
        mean = jnp.mean(mid, -1, keepdims=True)
        centred = mid - mean
        var = jnp.mean(centred * centred, -1, keepdims=True)
        source = (centred * lax.rsqrt(var + 1e-05) * gain_ref[...]).astype(jnp.bfloat16)
        source_ref[:, p] = source.reshape(2, HALF, LANES)
        sources.append(source)
    for half in range(2):
        proj = lax.dot_general(
            mapping_ref[half * 256 : (half + 1) * 256, :],
            jnp.concatenate(sources, axis=0),
            (((1,), (1,)), ((), ())),
            preferred_element_type=jnp.float32,
        )
        for p in range(rows):
            cover = cover_ref[pl.ds(step * rows + p, 1), :]
            gate = proj[:LANES, p * LANES : (p + 1) * LANES]
            value = proj[LANES:, p * LANES : (p + 1) * LANES]
            sides_ref[pl.ds(pl.multiple_of((half * 16 + step * rows + p) * LANES, LANES), LANES), :] = (
                cover * jax.nn.sigmoid(gate) * value
            )

    @pl.when(step == steps - 1)
    def _():
        def one(c, carry):
            sent_ref[c] = sides_ref[pl.ds(c, 32, stride=LANES), :].astype(jnp.bfloat16)
            return carry

        lax.fori_loop(0, LANES, one, 0, unroll=8)


def triangle_kernel(taken_ref, product_ref):
    low = lane_index((256, LANES)) < HALF
    sides = []
    for top in (0, 16):
        columns = []
        for q in range(4):
            even = taken_ref[:, 2 * q, top : top + 16, :].reshape(256, LANES).astype(jnp.float32)
            odd = taken_ref[:, 2 * q + 1, top : top + 16, :].reshape(256, LANES).astype(jnp.float32)
            first = jnp.where(low, even, pltpu.roll(odd, HALF, 1)).astype(jnp.bfloat16)
            second = jnp.where(low, pltpu.roll(even, HALF, 1), odd).astype(jnp.bfloat16)
            columns.append(
                jnp.concatenate(
                    [first.reshape(16, 1, 16, LANES), second.reshape(16, 1, 16, LANES)], axis=1
                ).reshape(512, LANES)
            )
        sides.append(jnp.concatenate(columns, axis=1))
    product = lax.dot_general(
        sides[0], sides[1], (((1,), (1,)), ((), ())), preferred_element_type=jnp.float32
    )
    product = product.reshape(16, 2, 16, 512)
    for q in range(4):
        first = product[:, 0, :, q * LANES : (q + 1) * LANES].reshape(256, LANES)
        second = product[:, 1, :, q * LANES : (q + 1) * LANES].reshape(256, LANES)
        product_ref[:, 2 * q] = (
            jnp.where(low, first, pltpu.roll(second, HALF, 1))
            .astype(jnp.bfloat16)
            .reshape(16, 16, LANES)
        )
        product_ref[:, 2 * q + 1] = (
            jnp.where(low, pltpu.roll(first, HALF, 1), second)
            .astype(jnp.bfloat16)
            .reshape(16, 16, LANES)
        )


def finish_kernel(
    product_ref, mid_ref, source_ref, gate_ref, final_ref, gain_ref, out_ref, normal_ref
):
    step = pl.program_id(0)
    rows = 4

    @pl.when(step == 0)
    def _():
        total = product_ref[0].astype(jnp.float32)
        for c in range(1, LANES):
            total = total + product_ref[c].astype(jnp.float32)
        mean = total / LANES
        square = jnp.zeros_like(mean)
        for c in range(LANES):
            centred = product_ref[c].astype(jnp.float32) - mean
            square = square + centred * centred
        scale = lax.rsqrt(square / LANES + 1e-05)
        for c in range(LANES):
            normal_ref[c * 16 : (c + 1) * 16, :] = (
                product_ref[c].astype(jnp.float32) - mean
            ) * scale

    for p in range(rows):
        centred = (
            normal_ref[pl.ds(step * rows + p, LANES, stride=16), :] * gain_ref[...]
        ).astype(jnp.bfloat16)
        result = lax.dot_general(
            centred, final_ref[...], (((0,), (0,)), ((), ())), preferred_element_type=jnp.float32
        )
        gate = jax.nn.sigmoid(
            jnp.dot(
                source_ref[:, p].reshape(LANES, LANES),
                gate_ref[...],
                preferred_element_type=jnp.float32,
            )
        )
        out_ref[:, p] = mid_ref[:, p] + (gate * result).reshape(2, HALF, LANES)


def whole(shape):
    return pl.BlockSpec(shape, lambda t: (0,) * len(shape), pipeline_mode=pl.Buffered(1))


def by_rows(dtype_rows=4):
    return pl.BlockSpec((2, dtype_rows, HALF, LANES), lambda t: (0, t, 0, 0))


PARAMS = pltpu.CompilerParams(
    vmem_limit_bytes=VMEM_LIMIT, dimension_semantics=("arbitrary",)
)


def pair_call(left, right, final, couple, cover, same, table, gain, mapping):
    return pl.pallas_call(
        pair_kernel,
        grid=(4,),
        in_specs=[
            pl.BlockSpec((1024, LANES), lambda t: (0, t)),
            pl.BlockSpec((1024, LANES), lambda t: (0, t + 4)),
            pl.BlockSpec((1024, LANES), lambda t: (0, 8), pipeline_mode=pl.Buffered(1)),
            whole((1024, 2176)),
            whole((256, 512)),
            by_rows(),
            whole((16, LANES)),
            whole((16, LANES)),
            whole((LANES, 2)),
            whole((1, LANES)),
            whole((512, LANES)),
        ],
        out_specs=[by_rows(), by_rows(), whole((LANES, 32, LANES))],
        out_shape=[
            jax.ShapeDtypeStruct((2, 16, HALF, LANES), jnp.float32),
            jax.ShapeDtypeStruct((2, 16, HALF, LANES), jnp.bfloat16),
            jax.ShapeDtypeStruct((LANES, 32, LANES), jnp.bfloat16),
        ],
        scratch_shapes=[
            pltpu.VMEM((256, 2048), jnp.bfloat16),
            pltpu.VMEM((16, LANES), jnp.float32),
            pltpu.VMEM((32 * LANES, LANES), jnp.float32),
        ],
        compiler_params=PARAMS,
        name="pair",
    )(left, left, left, right, final, couple, cover, same, table, gain, mapping)


def triangle_call(taken):
    return pl.pallas_call(
        triangle_kernel,
        out_shape=jax.ShapeDtypeStruct((16, 8, 16, LANES), jnp.bfloat16),
        compiler_params=pltpu.CompilerParams(vmem_limit_bytes=VMEM_LIMIT),
        name="triangle",
    )(taken)


def finish_call(product, mid, source, gate, final, gain):
    return pl.pallas_call(
        finish_kernel,
        grid=(4,),
        in_specs=[
            whole((LANES, 16, LANES)),
            by_rows(),
            by_rows(),
            whole((LANES, LANES)),
            whole((LANES, LANES)),
            whole((LANES, 1)),
        ],
        out_specs=by_rows(),
        out_shape=jax.ShapeDtypeStruct((2, 16, HALF, LANES), jnp.float32),
        scratch_shapes=[pltpu.VMEM((LANES * 16, LANES), jnp.float32)],
        compiler_params=PARAMS,
        name="finish",
    )(product, mid, source, gate, final, gain)


def spread_left(left, cover):
    row, n_row, n_col = lax.axis_index("row"), lax.axis_size("row"), lax.axis_size("col")
    halves = [
        jnp.concatenate(
            [
                left[:, h * 1024 : (h + 1) * 1024],
                jnp.pad(cover[:, h * 32 : (h + 1) * 32], ((0, 0), (0, LANES - 32))),
            ],
            axis=1,
        )
        for h in range(2)
    ]
    odd = row % 2 == 1
    own = jnp.where(odd, halves[1], halves[0])
    other = jnp.where(odd, halves[0], halves[1])

    def route(flip):
        return [
            (r * n_col + c, (2 * c + (r + flip) % 2) * n_col + r // 2)
            for r in range(n_row)
            for c in range(n_col)
        ]

    own = lax.ppermute(own, ("row", "col"), route(0))
    other = lax.ppermute(other, ("row", "col"), route(1))
    both = jnp.concatenate([jnp.where(odd, other, own), jnp.where(odd, own, other)], axis=0)
    return lax.all_gather(both, "col", axis=0, tiled=True)


def halves_on_lanes(grid):
    return jnp.concatenate([grid[:16], grid[16:]], axis=1)


def local(
    alignment_tensor,
    supplement_align_cover,
    couple_tensor,
    couple_cover_grid,
    amino_strand_label,
    focus_scaling_vector,
    focus_asking_factor,
    focus_lookup_factor,
    focus_content_factor,
    focus_sigmoid_factor,
    focus_final_factor,
    dyadic_scaling_vector,
    dyadic_first_factor,
    dyadic_second_factor,
    dyadic_final_factor,
    strand_couple_table,
    trio_source_scaling,
    trio_mapping_factors,
    trio_sigmoid_factor,
    trio_middle_scaling,
    trio_final_factor,
):
    hi = lax.Precision.HIGHEST
    n_row = lax.axis_size("row")
    n_col = lax.axis_size("col")
    alignments_each_device, vertical_aminos = supplement_align_cover.shape
    rows_res = couple_tensor.shape[0]
    align_feature_length = focus_scaling_vector.shape[0]
    head_dim = focus_lookup_factor.shape[1]
    heads = focus_asking_factor.shape[1] // head_dim
    width_o = dyadic_first_factor.shape[1]
    width_z = couple_tensor.shape[2]
    width_t = trio_final_factor.shape[0]
    split_cover_lines = supplement_align_cover.astype(jnp.bfloat16)
    dispatched, sent_mask = (
        lax.all_to_all(alignment_tensor, "row", split_axis=1, concat_axis=0, tiled=True),
        lax.all_to_all(split_cover_lines, "row", split_axis=1, concat_axis=0, tiled=True),
    )
    alignments_total, amino_swap = sent_mask.shape
    align_verticals = dispatched.reshape(alignments_total, amino_swap, align_feature_length).astype(
        jnp.float32
    )
    covered_contents = sent_mask.astype(jnp.float32)
    focus_source = standardize_features(align_verticals, focus_scaling_vector).astype(jnp.bfloat16)
    counts = jnp.maximum(jnp.sum(covered_contents, 0), 1.0)
    query_mean = (
        jnp.sum(covered_contents[:, :, None] * focus_source.astype(jnp.float32), 0)
        / counts[:, None]
    ).astype(jnp.bfloat16)
    query = (
        jnp.dot(query_mean, focus_asking_factor, preferred_element_type=jnp.float32)
        * head_dim ** (-0.5)
    ).reshape(amino_swap, heads, head_dim)
    flattened_source = focus_source.reshape(alignments_total * amino_swap, align_feature_length)
    keys = jnp.dot(
        flattened_source, focus_lookup_factor, preferred_element_type=jnp.float32
    ).reshape(alignments_total, amino_swap, head_dim)
    values = jnp.dot(
        flattened_source, focus_content_factor, preferred_element_type=jnp.float32
    ).reshape(alignments_total, amino_swap, head_dim)
    logits = jnp.einsum("rhd,srd->rhs", query, keys, precision=hi)
    logits = logits + jnp.where(covered_contents.T[:, None, :] > 0, 0.0, -1000000000.0).astype(
        jnp.float32
    )
    weights = jax.nn.softmax(logits, -1)
    mixed = jnp.einsum("rhs,srd->rhd", weights, values, precision=hi).reshape(
        amino_swap, heads * head_dim
    )
    gates = jax.nn.sigmoid(
        jnp.dot(flattened_source, focus_sigmoid_factor, preferred_element_type=jnp.float32)
    ).reshape(alignments_total, amino_swap, heads * head_dim)
    sigmoid_scaled_result = (
        (gates * mixed[None])
        .astype(jnp.bfloat16)
        .reshape(alignments_total * amino_swap, heads * head_dim)
    )
    refreshed = (
        align_verticals
        + jnp.dot(
            sigmoid_scaled_result, focus_final_factor, preferred_element_type=jnp.float32
        ).reshape(alignments_total, amino_swap, align_feature_length)
    ).astype(jnp.bfloat16)
    refreshed_supplement_align = lax.all_to_all(
        refreshed.reshape(alignments_total, amino_swap * align_feature_length),
        "row",
        split_axis=0,
        concat_axis=1,
        tiled=True,
    )
    device_align_slice = alignment_tensor.reshape(
        alignments_each_device, vertical_aminos, align_feature_length
    ).astype(jnp.float32)
    device_cover_slice = supplement_align_cover.astype(jnp.float32)
    product_source = (
        standardize_features(device_align_slice, dyadic_scaling_vector)
        .astype(jnp.bfloat16)
        .reshape(alignments_each_device * vertical_aminos, align_feature_length)
    )
    left = (
        (
            jnp.dot(
                product_source, dyadic_first_factor, preferred_element_type=jnp.float32
            ).reshape(alignments_each_device, vertical_aminos, width_o)
            * device_cover_slice[:, :, None]
        )
        .astype(jnp.bfloat16)
        .reshape(alignments_each_device, vertical_aminos * width_o)
    )
    right = (
        (
            jnp.dot(
                product_source, dyadic_second_factor, preferred_element_type=jnp.float32
            ).reshape(alignments_each_device, vertical_aminos, width_o)
            * device_cover_slice[:, :, None]
        )
        .astype(jnp.bfloat16)
        .transpose(0, 2, 1)
        .reshape(alignments_each_device, vertical_aminos * width_o)
    )
    right = jnp.concatenate([right, split_cover_lines, split_cover_lines], axis=1)
    left_rows = spread_left(left, split_cover_lines)
    right_all = lax.all_gather(right, "row", axis=0, tiled=True)
    chain_rows = lax.dynamic_slice_in_dim(
        amino_strand_label, lax.axis_index("row") * rows_res, rows_res, 0
    )
    chain_cols = lax.dynamic_slice_in_dim(
        amino_strand_label, lax.axis_index("col") * vertical_aminos, vertical_aminos, 0
    )
    same = (chain_rows[:, None] == chain_cols[None, :]).astype(jnp.float32)
    final = (
        dyadic_final_factor.reshape(width_o, 16, 2, width_z)
        .transpose(2, 3, 1, 0)
        .reshape(2 * width_z, 16 * width_o)
    )
    pair_mid, tri_in, sides = pair_call(
        left_rows,
        right_all,
        final,
        couple_tensor.reshape(2, 16, vertical_aminos, width_z),
        halves_on_lanes(couple_cover_grid.astype(jnp.float32)),
        halves_on_lanes(same),
        strand_couple_table.T,
        trio_source_scaling.reshape(1, width_z),
        trio_mapping_factors.T,
    )
    taken = lax.all_to_all(sides, ("row", "col"), 0, 0, tiled=True)
    product = triangle_call(taken.reshape(n_row, n_col, 32, LANES))
    product = lax.all_to_all(
        product.reshape(n_row * n_col, 16, LANES), ("row", "col"), 0, 0, tiled=True
    )
    refreshed_couple_tensor = finish_call(
        product,
        pair_mid,
        tri_in,
        trio_sigmoid_factor,
        trio_final_factor,
        trio_middle_scaling.reshape(width_t, 1),
    ).reshape(rows_res, vertical_aminos, width_z)
    return (refreshed_supplement_align, refreshed_couple_tensor)


def solution(mesh):
    in_specs = (
        P("row", "col"),
        P("row", "col"),
        P("row", "col", None),
        P("row", "col"),
        P(),
        P(),
        P(),
        P(),
        P(),
        P(),
        P(),
        P(),
        P(),
        P(),
        P(),
        P(),
        P(),
        P(),
        P(),
        P(),
        P(),
    )
    out_specs = (P("row", "col"), P("row", "col", None))
    return jax.shard_map(local, mesh=mesh, in_specs=in_specs, out_specs=out_specs, check_vma=False)
```

```python
import jax
import jax.numpy as jnp
from jax import lax
from jax.experimental import pallas as pl
from jax.experimental.pallas import tpu as pltpu
from jax.sharding import PartitionSpec as P

LANES = 128
HALF = 64
PART_ROWS = 40
VMEM_LIMIT = 50 * 1024 * 1024


def row_index(shape):
    return lax.broadcasted_iota(jnp.int32, shape, 0)


def ones_where(keep):
    return jnp.where(keep, 1.0, 0.0).astype(jnp.bfloat16)


def repeat_lanes(w, times):
    b = w.shape[1]
    shape = (b, times * b)
    pick = ones_where(lane_index(shape) % b == row_index(shape))
    return jnp.dot(w, pick, preferred_element_type=jnp.float32).astype(jnp.bfloat16)


def block_diagonal(w, times):
    a, b = w.shape
    tall = jnp.concatenate([repeat_lanes(w, times)] * times, axis=0)
    keep = row_index(tall.shape) // a == lane_index(tall.shape) // b
    return jnp.where(keep, tall, jnp.zeros_like(tall))


def parts_of(x, count):
    out = []
    for _ in range(count):
        part = x.astype(jnp.bfloat16)
        out.append(part)
        x = x - part.astype(jnp.float32)
    return out


def project_kernel(
    msa_ref,
    cover_ref,
    focus_gain_ref,
    dyadic_gain_ref,
    first_ref,
    second_ref,
    left_ref,
    right_ref,
    source_ref,
    sums_ref,
    turn_ref,
):
    odd = lax.axis_index("row") % 2
    cover = cover_ref[...].astype(jnp.float32)
    cover_narrow = cover.astype(jnp.bfloat16)
    cover_turned = jnp.concatenate([cover, cover], axis=0).T
    square = (256, 256)
    average = jnp.where(
        row_index(square) // HALF == lane_index(square) // HALF, 1.0 / HALF, 0.0
    ).astype(jnp.bfloat16)
    first = block_diagonal(first_ref[...], 4)
    second = block_diagonal(second_ref[...], 4)
    focus_gain = jnp.concatenate([focus_gain_ref[...]] * 4, axis=1)
    dyadic_gain = jnp.concatenate([dyadic_gain_ref[...]] * 4, axis=1)
    for q in range(4):
        x = jnp.concatenate(
            [msa_ref[:, (4 * q + e) * 256 : (4 * q + e + 1) * 256] for e in range(4)], axis=0
        )
        mean = jnp.dot(x, average, preferred_element_type=jnp.float32)
        centred = x.astype(jnp.float32) - mean
        high, low = parts_of(centred * centred, 2)
        var = jnp.dot(high, average, preferred_element_type=jnp.float32) + jnp.dot(
            low, average, preferred_element_type=jnp.float32
        )
        normal = centred * lax.rsqrt(var + 1e-05)
        focus = (normal * focus_gain).astype(jnp.bfloat16)
        dyadic = (normal * dyadic_gain).astype(jnp.bfloat16)
        source_ref[q * 256 : (q + 1) * 256, :] = focus
        left = lax.dot_general(
            dyadic, first, (((1,), (1,)), ((), ())), preferred_element_type=jnp.float32
        )
        pick = ones_where(row_index((64, 512)) == 16 * q + lane_index((64, 512)) // 32)
        left_cover = jnp.dot(cover_narrow, pick, preferred_element_type=jnp.float32)
        right = lax.dot_general(
            second, dyadic, (((1,), (1,)), ((), ())), preferred_element_type=jnp.float32
        )
        pick = ones_where(row_index((64, 1024)) == 16 * q + lane_index((64, 1024)) // 64)
        focus_cover = jnp.dot(cover_narrow, pick, preferred_element_type=jnp.float32)
        for e in range(4):
            g = 4 * q + e
            rows = slice(e * HALF, (e + 1) * HALF)
            left_ref[(g // 8 + odd) % 2, :, (g % 8) * LANES : (g % 8 + 1) * LANES] = (
                left[rows] * left_cover[:, e * LANES : (e + 1) * LANES]
            ).astype(jnp.bfloat16)
            here = right[:, (e // 2) * LANES : (e // 2 + 1) * LANES]
            if e % 2:
                here = pltpu.roll(here, HALF, 1)
            for j in range(4):
                turn_ref[pl.ds(4 * g + j, 32, stride=HALF), :] = (
                    here[j * 32 : (j + 1) * 32] * cover_turned[4 * g + j : 4 * g + j + 1, :]
                )
            wide = focus_cover[:, e * 256 : (e + 1) * 256]
            total = jnp.sum(wide * focus[rows].astype(jnp.float32), 0, keepdims=True)
            count = jnp.sum(wide, 0, keepdims=True)
            for k in range(16):
                sums_ref[k, g : g + 1, :] = total
                sums_ref[k, 16 + g : 17 + g, :] = count
    shape = (64, LANES)
    for h in range(2):
        pick = ones_where(
            (row_index(shape) == 32 * h + lane_index(shape)) & (lane_index(shape) < 32)
        )
        left_ref[(h + odd) % 2, :, 1024:1152] = jnp.dot(
            cover_narrow, pick, preferred_element_type=jnp.float32
        ).astype(jnp.bfloat16)
    pick = ones_where(row_index(shape) == lane_index(shape) % HALF)
    right_ref[:, 2048:2176] = jnp.dot(
        cover_narrow, pick, preferred_element_type=jnp.float32
    ).astype(jnp.bfloat16)
    for d in range(16):
        turned = turn_ref[d * LANES : (d + 1) * LANES, :].T
        right_ref[:, d * LANES : (d + 1) * LANES] = turned[:HALF].astype(jnp.bfloat16)


def attend_kernel(source_ref, cover_ref, sums_ref, asking_ref, lookup_ref, content_ref, part_ref):
    sums = sums_ref[0]
    for k in range(1, 16):
        sums = sums + sums_ref[k]
    query_mean = (sums[:16] / jnp.maximum(sums[16:], 1.0)).astype(jnp.bfloat16)
    query = (
        jnp.dot(query_mean, block_diagonal(asking_ref[...], 4), preferred_element_type=jnp.float32)
        * 8 ** (-0.5)
    )
    shape = (512, 256)
    spread = jnp.concatenate([jnp.broadcast_to(query[g : g + 1], (32, 256)) for g in range(16)], 0)
    spread = jnp.where(row_index(shape) % 32 == lane_index(shape) // 8, spread, 0.0)
    lookup = jnp.concatenate([lookup_ref[...].astype(jnp.float32)] * 8, axis=0)
    lookup = block_diagonal(lookup.astype(jnp.bfloat16), 4)
    ask = sum(
        jnp.dot(part, lookup, preferred_element_type=jnp.float32) for part in parts_of(spread, 3)
    )
    ask_parts = parts_of(ask, 3)
    logits = []
    for g in range(16):
        stacked = jnp.concatenate([part[g * 32 : (g + 1) * 32] for part in ask_parts], axis=0)
        three = lax.dot_general(
            stacked,
            source_ref[g * HALF : (g + 1) * HALF, :],
            (((1,), (1,)), ((), ())),
            preferred_element_type=jnp.float32,
        )
        logits.append(three[:32] + three[32:64] + three[64:])
    logits = jnp.concatenate(logits, axis=0)
    cover = cover_ref[...].astype(jnp.float32).T
    bias = jnp.where(cover > 0, 0.0, -1000000000.0)
    logits = logits + jnp.broadcast_to(bias[:, None, :], (64, 8, 64)).reshape(512, 64)
    top = jnp.max(logits, 1, keepdims=True)
    weights = jnp.exp(logits - top)
    total = jnp.sum(weights, 1, keepdims=True)
    weight_parts = parts_of(weights, 3)
    mixed = []
    for g in range(16):
        stacked = jnp.concatenate([part[g * 32 : (g + 1) * 32] for part in weight_parts], axis=0)
        three = jnp.dot(
            stacked, source_ref[g * HALF : (g + 1) * HALF, :], preferred_element_type=jnp.float32
        )
        mixed.append(three[:32] + three[32:64] + three[64:])
    mixed = jnp.concatenate(mixed, axis=0)
    mixed = jnp.where(row_index(shape) // 8 % 4 == lane_index(shape) // HALF, mixed, 0.0)
    small = (8, LANES)
    content = lax.dot_general(
        content_ref[...],
        ones_where(lane_index(small) == row_index(small) + 8),
        (((0,), (0,)), ((), ())),
        preferred_element_type=jnp.float32,
    ).astype(jnp.bfloat16)
    content = jnp.concatenate([content] * 4, axis=0)
    mixed = sum(
        jnp.dot(part, content, preferred_element_type=jnp.float32) for part in parts_of(mixed, 3)
    )
    lane = lane_index((512, LANES))
    mixed = jnp.where(lane == 0, top, jnp.where(lane == 1, total, mixed))
    part_ref[...] = mixed.T[:PART_ROWS]


def refresh_kernel(part_ref, source_ref, msa_ref, sigmoid_ref, final_ref, out_ref):
    parts = [part_ref[k * PART_ROWS : k * PART_ROWS + 16, :] for k in range(16)]
    top = parts[0][0:1]
    for k in range(1, 16):
        top = jnp.maximum(top, parts[k][0:1])
    merged = jnp.zeros((16, 512), jnp.float32)
    for k in range(16):
        merged = merged + parts[k] * jnp.exp(parts[k][0:1] - top)
    mixed = merged[8:] / merged[1:2]
    shape = (LANES, 1024)
    spread = ones_where(row_index(shape) == lane_index(shape) // 8)
    keep = row_index((8, 1024)) == lane_index((8, 1024)) % 8
    gate_weight = block_diagonal(sigmoid_ref[...], 4)
    final_weight = block_diagonal(final_ref[...], 4)
    for q in range(4):
        stacked = jnp.concatenate(parts_of(mixed[:, q * LANES : (q + 1) * LANES], 3), axis=0)
        three = jnp.dot(stacked, spread, preferred_element_type=jnp.float32)
        wide = jnp.where(keep, three[:8] + three[8:16] + three[16:], 0.0)
        wide = jnp.sum(wide, 0, keepdims=True)
        wide = jnp.concatenate(
            [jnp.broadcast_to(wide[:, e * 256 : (e + 1) * 256], (HALF, 256)) for e in range(4)],
            axis=0,
        )
        gate = jax.nn.sigmoid(
            jnp.dot(
                source_ref[q * 256 : (q + 1) * 256, :],
                gate_weight,
                preferred_element_type=jnp.float32,
            )
        )
        change = jnp.dot(
            (gate * wide).astype(jnp.bfloat16), final_weight, preferred_element_type=jnp.float32
        )
        for e in range(4):
            lanes = slice((4 * q + e) * 256, (4 * q + e + 1) * 256)
            out_ref[:, lanes] = (
                msa_ref[:, lanes].astype(jnp.float32) + change[e * HALF : (e + 1) * HALF]
            ).astype(jnp.bfloat16)


def lane_index(shape):
    return lax.broadcasted_iota(jnp.int32, shape, len(shape) - 1)


def pair_kernel(
    left_a_ref,
    left_b_ref,
    left_mask_ref,
    right_ref,
    final_ref,
    couple_ref,
    cover_ref,
    same_ref,
    table_ref,
    gain_ref,
    mapping_ref,
    mid_ref,
    source_ref,
    sent_ref,
    outer_ref,
    count_ref,
    sides_ref,
):
    step = pl.program_id(0)
    steps = pl.num_programs(0)
    rows = 4
    low = lane_index((LANES, LANES)) < HALF
    odd = lax.axis_index("row") % 2
    col = lax.axis_index("col")

    def in_order(ref):
        blocks = []
        for block in range(16):
            turn = (block // 4 - col // 2 + 4) % 4
            place = jnp.where(turn == 2, 3, jnp.where(turn == 3, 1, jnp.where(turn == 1, 2, 0)))
            other = (block // 2 + col) % 2
            start = other * 512 + place * 128 + (block + odd) % 2 * 64
            blocks.append(ref[pl.ds(pl.multiple_of(start, HALF), HALF), :])
        return jnp.concatenate(blocks, axis=0)

    @pl.when(step == 0)
    def _():
        both = lax.dot_general(
            in_order(left_mask_ref),
            right_ref[:, 2048:2176],
            (((0,), (0,)), ((), ())),
            preferred_element_type=jnp.float32,
        )
        both = jnp.maximum(both[:32], 1.0)
        count_ref[...] = jnp.where(lane_index((16, LANES)) < HALF, both[:16], both[16:])

    left = jnp.concatenate([in_order(left_a_ref), in_order(left_b_ref)], axis=1).T
    for n in range(8):
        outer_ref[:, n * 256 : (n + 1) * 256] = jnp.dot(
            left, right_ref[:, n * 256 : (n + 1) * 256], preferred_element_type=jnp.float32
        ).astype(jnp.bfloat16)

    sources = []
    for p in range(rows):
        halves = []
        for top in (p * 32, 128 + p * 32):
            halves.append(
                jnp.concatenate(
                    [outer_ref[top : top + 32, d * LANES : (d + 1) * LANES] for d in range(16)],
                    axis=0,
                )
            )
        update = jnp.dot(
            final_ref[...],
            jnp.concatenate(halves, axis=1),
            preferred_element_type=jnp.float32,
        )
        a0, a1 = update[:LANES, :LANES], update[LANES:, :LANES]
        b0, b1 = update[:LANES, LANES:], update[LANES:, LANES:]
        update = jnp.where(low, a0, b1) + pltpu.roll(jnp.where(low, b0, a1), HALF, 1)
        here = pl.ds(step * rows + p, 1)
        update = update / count_ref[here, :]
        update = update + jnp.where(same_ref[here, :] > 0, table_ref[:, 1:2], table_ref[:, 0:1])
        mid = couple_ref[:, p].reshape(LANES, LANES) + update.T
        mid_ref[:, p] = mid.reshape(2, HALF, LANES)
        mean = jnp.mean(mid, -1, keepdims=True)
        centred = mid - mean
        var = jnp.mean(centred * centred, -1, keepdims=True)
        source = (centred * lax.rsqrt(var + 1e-05) * gain_ref[...]).astype(jnp.bfloat16)
        source_ref[:, p] = source.reshape(2, HALF, LANES)
        sources.append(source)
    for half in range(2):
        proj = lax.dot_general(
            mapping_ref[half * 256 : (half + 1) * 256, :],
            jnp.concatenate(sources, axis=0),
            (((1,), (1,)), ((), ())),
            preferred_element_type=jnp.float32,
        )
        for p in range(rows):
            cover = cover_ref[pl.ds(step * rows + p, 1), :]
            gate = proj[:LANES, p * LANES : (p + 1) * LANES]
            value = proj[LANES:, p * LANES : (p + 1) * LANES]
            sides_ref[pl.ds(pl.multiple_of((half * 16 + step * rows + p) * LANES, LANES), LANES), :] = (
                cover * jax.nn.sigmoid(gate) * value
            )

    @pl.when(step == steps - 1)
    def _():
        def one(c, carry):
            sent_ref[c] = sides_ref[pl.ds(c, 32, stride=LANES), :].astype(jnp.bfloat16)
            return carry

        lax.fori_loop(0, LANES, one, 0, unroll=8)


def triangle_kernel(taken_ref, product_ref):
    low = lane_index((256, LANES)) < HALF
    sides = []
    for top in (0, 16):
        columns = []
        for q in range(4):
            even = taken_ref[:, 2 * q, top : top + 16, :].reshape(256, LANES).astype(jnp.float32)
            odd = taken_ref[:, 2 * q + 1, top : top + 16, :].reshape(256, LANES).astype(jnp.float32)
            first = jnp.where(low, even, pltpu.roll(odd, HALF, 1)).astype(jnp.bfloat16)
            second = jnp.where(low, pltpu.roll(even, HALF, 1), odd).astype(jnp.bfloat16)
            columns.append(
                jnp.concatenate(
                    [first.reshape(16, 1, 16, LANES), second.reshape(16, 1, 16, LANES)], axis=1
                ).reshape(512, LANES)
            )
        sides.append(jnp.concatenate(columns, axis=1))
    product = lax.dot_general(
        sides[0], sides[1], (((1,), (1,)), ((), ())), preferred_element_type=jnp.float32
    )
    product = product.reshape(16, 2, 16, 512)
    for q in range(4):
        first = product[:, 0, :, q * LANES : (q + 1) * LANES].reshape(256, LANES)
        second = product[:, 1, :, q * LANES : (q + 1) * LANES].reshape(256, LANES)
        product_ref[:, 2 * q] = (
            jnp.where(low, first, pltpu.roll(second, HALF, 1))
            .astype(jnp.bfloat16)
            .reshape(16, 16, LANES)
        )
        product_ref[:, 2 * q + 1] = (
            jnp.where(low, pltpu.roll(first, HALF, 1), second)
            .astype(jnp.bfloat16)
            .reshape(16, 16, LANES)
        )


def finish_kernel(
    product_ref, mid_ref, source_ref, gate_ref, final_ref, gain_ref, out_ref, normal_ref
):
    step = pl.program_id(0)
    rows = 4

    @pl.when(step == 0)
    def _():
        total = product_ref[0].astype(jnp.float32)
        for c in range(1, LANES):
            total = total + product_ref[c].astype(jnp.float32)
        mean = total / LANES
        square = jnp.zeros_like(mean)
        for c in range(LANES):
            centred = product_ref[c].astype(jnp.float32) - mean
            square = square + centred * centred
        scale = lax.rsqrt(square / LANES + 1e-05)
        for c in range(LANES):
            normal_ref[c * 16 : (c + 1) * 16, :] = (
                product_ref[c].astype(jnp.float32) - mean
            ) * scale

    for p in range(rows):
        centred = (
            normal_ref[pl.ds(step * rows + p, LANES, stride=16), :] * gain_ref[...]
        ).astype(jnp.bfloat16)
        result = lax.dot_general(
            centred, final_ref[...], (((0,), (0,)), ((), ())), preferred_element_type=jnp.float32
        )
        gate = jax.nn.sigmoid(
            jnp.dot(
                source_ref[:, p].reshape(LANES, LANES),
                gate_ref[...],
                preferred_element_type=jnp.float32,
            )
        )
        out_ref[:, p] = mid_ref[:, p] + (gate * result).reshape(2, HALF, LANES)


def whole(shape):
    return pl.BlockSpec(shape, lambda t: (0,) * len(shape), pipeline_mode=pl.Buffered(1))


def by_rows(dtype_rows=4):
    return pl.BlockSpec((2, dtype_rows, HALF, LANES), lambda t: (0, t, 0, 0))


PARAMS = pltpu.CompilerParams(
    vmem_limit_bytes=VMEM_LIMIT, dimension_semantics=("arbitrary",)
)


def cost(us):
    return pl.CostEstimate(flops=us * 10**9, bytes_accessed=us * 10**6, transcendentals=0)


def pair_call(left, right, final, couple, cover, same, table, gain, mapping):
    return pl.pallas_call(
        pair_kernel,
        grid=(4,),
        in_specs=[
            pl.BlockSpec((1024, LANES), lambda t: (0, t)),
            pl.BlockSpec((1024, LANES), lambda t: (0, t + 4)),
            pl.BlockSpec((1024, LANES), lambda t: (0, 8), pipeline_mode=pl.Buffered(1)),
            whole((1024, 2176)),
            whole((256, 512)),
            by_rows(),
            whole((16, LANES)),
            whole((16, LANES)),
            whole((LANES, 2)),
            whole((1, LANES)),
            whole((512, LANES)),
        ],
        out_specs=[by_rows(), by_rows(), whole((LANES, 32, LANES))],
        out_shape=[
            jax.ShapeDtypeStruct((2, 16, HALF, LANES), jnp.float32),
            jax.ShapeDtypeStruct((2, 16, HALF, LANES), jnp.bfloat16),
            jax.ShapeDtypeStruct((LANES, 32, LANES), jnp.bfloat16),
        ],
        scratch_shapes=[
            pltpu.VMEM((256, 2048), jnp.bfloat16),
            pltpu.VMEM((16, LANES), jnp.float32),
            pltpu.VMEM((32 * LANES, LANES), jnp.float32),
        ],
        compiler_params=PARAMS,
        cost_estimate=cost(16),
        name="pair",
    )(left, left, left, right, final, couple, cover, same, table, gain, mapping)


def triangle_call(taken):
    return pl.pallas_call(
        triangle_kernel,
        out_shape=jax.ShapeDtypeStruct((16, 8, 16, LANES), jnp.bfloat16),
        compiler_params=pltpu.CompilerParams(vmem_limit_bytes=VMEM_LIMIT),
        cost_estimate=cost(2),
        name="triangle",
    )(taken)


def finish_call(product, mid, source, gate, final, gain):
    return pl.pallas_call(
        finish_kernel,
        grid=(4,),
        in_specs=[
            whole((LANES, 16, LANES)),
            by_rows(),
            by_rows(),
            whole((LANES, LANES)),
            whole((LANES, LANES)),
            whole((LANES, 1)),
        ],
        out_specs=by_rows(),
        out_shape=jax.ShapeDtypeStruct((2, 16, HALF, LANES), jnp.float32),
        scratch_shapes=[pltpu.VMEM((LANES * 16, LANES), jnp.float32)],
        compiler_params=PARAMS,
        cost_estimate=cost(3),
        name="finish",
    )(product, mid, source, gate, final, gain)


def project_call(msa, cover, focus_gain, dyadic_gain, first, second):
    return pl.pallas_call(
        project_kernel,
        out_shape=[
            jax.ShapeDtypeStruct((2, 64, 1152), jnp.bfloat16),
            jax.ShapeDtypeStruct((64, 2176), jnp.bfloat16),
            jax.ShapeDtypeStruct((1024, 256), jnp.bfloat16),
            jax.ShapeDtypeStruct((16, 32, 256), jnp.float32),
        ],
        scratch_shapes=[pltpu.VMEM((2048, LANES), jnp.float32)],
        compiler_params=pltpu.CompilerParams(vmem_limit_bytes=VMEM_LIMIT),
        cost_estimate=cost(4),
        name="project",
    )(msa, cover, focus_gain, dyadic_gain, first, second)


def attend_call(source, cover, sums, asking, lookup, content):
    return pl.pallas_call(
        attend_kernel,
        out_shape=jax.ShapeDtypeStruct((PART_ROWS, 512), jnp.float32),
        compiler_params=pltpu.CompilerParams(vmem_limit_bytes=VMEM_LIMIT),
        cost_estimate=cost(3),
        name="attend",
    )(source, cover, sums, asking, lookup, content)


def refresh_call(parts, source, msa, gate, final):
    return pl.pallas_call(
        refresh_kernel,
        out_shape=jax.ShapeDtypeStruct((64, 4096), jnp.bfloat16),
        compiler_params=pltpu.CompilerParams(vmem_limit_bytes=VMEM_LIMIT),
        cost_estimate=cost(2),
        name="refresh",
    )(parts, source, msa, gate, final)


def ring_of_four(block, axis, step):
    half = block.shape[0] // 2
    back = lax.ppermute(block, axis, step(1))
    ahead = lax.ppermute(block, axis, step(-1))
    opposite = [
        lax.ppermute(back[:half], axis, step(1)),
        lax.ppermute(ahead[half:], axis, step(-1)),
    ]
    return jnp.concatenate([block, back, ahead] + opposite, axis=0)


def spread_left(left):
    n_row, n_col = lax.axis_size("row"), lax.axis_size("col")

    def route(flip):
        return [
            (r * n_col + c, (2 * c + (r + flip) % 2) * n_col + r // 2)
            for r in range(n_row)
            for c in range(n_col)
        ]

    def along(step):
        return [(c, (c + 2 * step) % n_col) for c in range(n_col)]

    both = jnp.concatenate(
        [lax.ppermute(left[flip], ("row", "col"), route(flip)) for flip in range(2)], axis=0
    )
    gathered = ring_of_four(both, "col", along)
    swapped = lax.ppermute(gathered, "col", [(c, c ^ 1) for c in range(n_col)])
    return jnp.concatenate([gathered, swapped], axis=0)


def halves_on_lanes(grid):
    return jnp.concatenate([grid[:16], grid[16:]], axis=1)


def local(
    alignment_tensor,
    supplement_align_cover,
    couple_tensor,
    couple_cover_grid,
    amino_strand_label,
    focus_scaling_vector,
    focus_asking_factor,
    focus_lookup_factor,
    focus_content_factor,
    focus_sigmoid_factor,
    focus_final_factor,
    dyadic_scaling_vector,
    dyadic_first_factor,
    dyadic_second_factor,
    dyadic_final_factor,
    strand_couple_table,
    trio_source_scaling,
    trio_mapping_factors,
    trio_sigmoid_factor,
    trio_middle_scaling,
    trio_final_factor,
):
    n_row = lax.axis_size("row")
    n_col = lax.axis_size("col")
    vertical_aminos = supplement_align_cover.shape[1]
    rows_res = couple_tensor.shape[0]
    width_o = dyadic_first_factor.shape[1]
    width_z = couple_tensor.shape[2]
    width_t = trio_final_factor.shape[0]
    left, right, source, sums = project_call(
        alignment_tensor,
        supplement_align_cover,
        focus_scaling_vector.reshape(1, HALF),
        dyadic_scaling_vector.reshape(1, HALF),
        dyadic_first_factor.T,
        dyadic_second_factor.T,
    )
    right_all = lax.all_gather(right, "row", axis=0, tiled=True)
    sums = lax.all_to_all(sums, "row", 0, 0, tiled=True)
    left, sums = lax.optimization_barrier((left, sums))
    parts = attend_call(
        source,
        supplement_align_cover,
        sums,
        focus_asking_factor,
        focus_lookup_factor.T,
        focus_content_factor.T,
    )
    left_rows, parts = lax.optimization_barrier((spread_left(left), parts))
    parts = lax.all_gather(parts, "row", axis=0, tiled=True)
    refreshed_supplement_align = refresh_call(
        parts, source, alignment_tensor, focus_sigmoid_factor, focus_final_factor
    )
    chain_rows = lax.dynamic_slice_in_dim(
        amino_strand_label, lax.axis_index("row") * rows_res, rows_res, 0
    )
    chain_cols = lax.dynamic_slice_in_dim(
        amino_strand_label, lax.axis_index("col") * vertical_aminos, vertical_aminos, 0
    )
    same = (chain_rows[:, None] == chain_cols[None, :]).astype(jnp.float32)
    final = (
        dyadic_final_factor.reshape(width_o, 16, 2, width_z)
        .transpose(2, 3, 1, 0)
        .reshape(2 * width_z, 16 * width_o)
    )
    pair_mid, tri_in, sides = pair_call(
        left_rows,
        right_all,
        final,
        couple_tensor.reshape(2, 16, vertical_aminos, width_z),
        halves_on_lanes(couple_cover_grid.astype(jnp.float32)),
        halves_on_lanes(same),
        strand_couple_table.T,
        trio_source_scaling.reshape(1, width_z),
        trio_mapping_factors.T,
    )
    taken = lax.all_to_all(sides, ("row", "col"), 0, 0, tiled=True)
    product = triangle_call(taken.reshape(n_row, n_col, 32, LANES))
    product = lax.all_to_all(
        product.reshape(n_row * n_col, 16, LANES), ("row", "col"), 0, 0, tiled=True
    )
    refreshed_couple_tensor = finish_call(
        product,
        pair_mid,
        tri_in,
        trio_sigmoid_factor,
        trio_final_factor,
        trio_middle_scaling.reshape(width_t, 1),
    ).reshape(rows_res, vertical_aminos, width_z)
    return (refreshed_supplement_align, refreshed_couple_tensor)


def solution(mesh):
    in_specs = (
        P("row", "col"),
        P("row", "col"),
        P("row", "col", None),
        P("row", "col"),
        P(),
        P(),
        P(),
        P(),
        P(),
        P(),
        P(),
        P(),
        P(),
        P(),
        P(),
        P(),
        P(),
        P(),
        P(),
        P(),
        P(),
    )
    out_specs = (P("row", "col"), P("row", "col", None))
    return jax.shard_map(local, mesh=mesh, in_specs=in_specs, out_specs=out_specs, check_vma=False)
```

```python
import jax
import jax.numpy as jnp
from jax import lax
from jax.experimental import pallas as pl
from jax.experimental.pallas import tpu as pltpu
from jax.sharding import PartitionSpec as P

LANES = 128
HALF = 64
PART_ROWS = 40
VMEM_LIMIT = 50 * 1024 * 1024
ALL_VMEM = 64 * 1024 * 1024 - 8192


def row_index(shape):
    return lax.broadcasted_iota(jnp.int32, shape, 0)


def ones_where(keep):
    return jnp.where(keep, 1.0, 0.0).astype(jnp.bfloat16)


def repeat_lanes(w, times):
    b = w.shape[1]
    shape = (b, times * b)
    pick = ones_where(lane_index(shape) % b == row_index(shape))
    return jnp.dot(w, pick, preferred_element_type=jnp.float32).astype(jnp.bfloat16)


def block_diagonal(w, times):
    a, b = w.shape
    tall = jnp.concatenate([repeat_lanes(w, times)] * times, axis=0)
    keep = row_index(tall.shape) // a == lane_index(tall.shape) // b
    return jnp.where(keep, tall, jnp.zeros_like(tall))


def parts_of(x, count):
    out = []
    for _ in range(count):
        part = x.astype(jnp.bfloat16)
        out.append(part)
        x = x - part.astype(jnp.float32)
    return out


def project_kernel(
    msa_ref,
    cover_ref,
    focus_gain_ref,
    dyadic_gain_ref,
    first_ref,
    second_ref,
    left_ref,
    right_ref,
    source_ref,
    sums_ref,
    turn_ref,
):
    odd = lax.axis_index("row") % 2
    cover = cover_ref[...].astype(jnp.float32)
    cover_narrow = cover.astype(jnp.bfloat16)
    cover_turned = jnp.concatenate([cover, cover], axis=0).T
    square = (256, 256)
    average = jnp.where(
        row_index(square) // HALF == lane_index(square) // HALF, 1.0 / HALF, 0.0
    ).astype(jnp.bfloat16)
    first = block_diagonal(first_ref[...], 4)
    second = block_diagonal(second_ref[...], 4)
    focus_gain = jnp.concatenate([focus_gain_ref[...]] * 4, axis=1)
    dyadic_gain = jnp.concatenate([dyadic_gain_ref[...]] * 4, axis=1)
    for q in range(4):
        x = jnp.concatenate(
            [msa_ref[:, (4 * q + e) * 256 : (4 * q + e + 1) * 256] for e in range(4)], axis=0
        )
        mean = jnp.dot(x, average, preferred_element_type=jnp.float32)
        centred = x.astype(jnp.float32) - mean
        high, low = parts_of(centred * centred, 2)
        var = jnp.dot(high, average, preferred_element_type=jnp.float32) + jnp.dot(
            low, average, preferred_element_type=jnp.float32
        )
        normal = centred * lax.rsqrt(var + 1e-05)
        focus = (normal * focus_gain).astype(jnp.bfloat16)
        dyadic = (normal * dyadic_gain).astype(jnp.bfloat16)
        source_ref[q * 256 : (q + 1) * 256, :] = focus
        left = lax.dot_general(
            dyadic, first, (((1,), (1,)), ((), ())), preferred_element_type=jnp.float32
        )
        pick = ones_where(row_index((64, 512)) == 16 * q + lane_index((64, 512)) // 32)
        left_cover = jnp.dot(cover_narrow, pick, preferred_element_type=jnp.float32)
        right = lax.dot_general(
            second, dyadic, (((1,), (1,)), ((), ())), preferred_element_type=jnp.float32
        )
        pick = ones_where(row_index((64, 1024)) == 16 * q + lane_index((64, 1024)) // 64)
        focus_cover = jnp.dot(cover_narrow, pick, preferred_element_type=jnp.float32)
        for e in range(4):
            g = 4 * q + e
            rows = slice(e * HALF, (e + 1) * HALF)
            left_ref[(g // 8 + odd) % 2, :, (g % 8) * LANES : (g % 8 + 1) * LANES] = (
                left[rows] * left_cover[:, e * LANES : (e + 1) * LANES]
            ).astype(jnp.bfloat16)
            here = right[:, (e // 2) * LANES : (e // 2 + 1) * LANES]
            if e % 2:
                here = pltpu.roll(here, HALF, 1)
            for j in range(4):
                turn_ref[pl.ds(4 * g + j, 32, stride=HALF), :] = (
                    here[j * 32 : (j + 1) * 32] * cover_turned[4 * g + j : 4 * g + j + 1, :]
                )
            wide = focus_cover[:, e * 256 : (e + 1) * 256]
            total = jnp.sum(wide * focus[rows].astype(jnp.float32), 0, keepdims=True)
            for k in range(16):
                sums_ref[k, g : g + 1, :] = total
    count = jnp.sum(cover, 0, keepdims=True)
    for k in range(16):
        sums_ref[k, 16:, :] = jnp.zeros((8, 256), jnp.float32)
        sums_ref[k, 16:17, :HALF] = count
    shape = (64, LANES)
    for h in range(2):
        pick = ones_where(
            (row_index(shape) == 32 * h + lane_index(shape)) & (lane_index(shape) < 32)
        )
        left_ref[(h + odd) % 2, :, 1024:1152] = jnp.dot(
            cover_narrow, pick, preferred_element_type=jnp.float32
        ).astype(jnp.bfloat16)
    pick = ones_where(row_index(shape) == lane_index(shape) % HALF)
    right_ref[:, 2048:2176] = jnp.dot(
        cover_narrow, pick, preferred_element_type=jnp.float32
    ).astype(jnp.bfloat16)
    for d in range(16):
        turned = turn_ref[d * LANES : (d + 1) * LANES, :].T
        right_ref[:, d * LANES : (d + 1) * LANES] = turned[:HALF].astype(jnp.bfloat16)


def attend_kernel(source_ref, cover_ref, sums_ref, asking_ref, lookup_ref, content_ref, part_ref):
    sums = sums_ref[0]
    for k in range(1, 16):
        sums = sums + sums_ref[k]
    count = jnp.broadcast_to(sums[16:17, :HALF], (16, HALF))
    shape = (16, HALF)
    count = jnp.where(lane_index(shape) // 4 == row_index(shape), count, 0.0)
    shape = (HALF, 256)
    pick = ones_where(row_index(shape) % 4 == lane_index(shape) // HALF)
    count = sum(
        jnp.dot(part, pick, preferred_element_type=jnp.float32) for part in parts_of(count, 2)
    )
    query_mean = (sums[:16] / jnp.maximum(count, 1.0)).astype(jnp.bfloat16)
    query = (
        jnp.dot(query_mean, block_diagonal(asking_ref[...], 4), preferred_element_type=jnp.float32)
        * 8 ** (-0.5)
    )
    shape = (512, 256)
    spread = jnp.concatenate([jnp.broadcast_to(query[g : g + 1], (32, 256)) for g in range(16)], 0)
    spread = jnp.where(row_index(shape) % 32 == lane_index(shape) // 8, spread, 0.0)
    lookup = jnp.concatenate([lookup_ref[...].astype(jnp.float32)] * 8, axis=0)
    lookup = block_diagonal(lookup.astype(jnp.bfloat16), 4)
    ask = sum(
        jnp.dot(part, lookup, preferred_element_type=jnp.float32) for part in parts_of(spread, 3)
    )
    ask_parts = parts_of(ask, 3)
    logits = []
    for g in range(16):
        stacked = jnp.concatenate([part[g * 32 : (g + 1) * 32] for part in ask_parts], axis=0)
        three = lax.dot_general(
            stacked,
            source_ref[g * HALF : (g + 1) * HALF, :],
            (((1,), (1,)), ((), ())),
            preferred_element_type=jnp.float32,
        )
        logits.append(three[:32] + three[32:64] + three[64:])
    logits = jnp.concatenate(logits, axis=0)
    cover = cover_ref[...].astype(jnp.float32).T
    bias = jnp.where(cover > 0, 0.0, -1000000000.0)
    logits = logits + jnp.broadcast_to(bias[:, None, :], (64, 8, 64)).reshape(512, 64)
    top = jnp.max(logits, 1, keepdims=True)
    weights = jnp.exp(logits - top)
    total = jnp.sum(weights, 1, keepdims=True)
    weight_parts = parts_of(weights, 3)
    mixed = []
    for g in range(16):
        stacked = jnp.concatenate([part[g * 32 : (g + 1) * 32] for part in weight_parts], axis=0)
        three = jnp.dot(
            stacked, source_ref[g * HALF : (g + 1) * HALF, :], preferred_element_type=jnp.float32
        )
        mixed.append(three[:32] + three[32:64] + three[64:])
    mixed = jnp.concatenate(mixed, axis=0)
    mixed = jnp.where(row_index(shape) // 8 % 4 == lane_index(shape) // HALF, mixed, 0.0)
    small = (8, LANES)
    content = lax.dot_general(
        content_ref[...],
        ones_where(lane_index(small) == row_index(small) + 8),
        (((0,), (0,)), ((), ())),
        preferred_element_type=jnp.float32,
    ).astype(jnp.bfloat16)
    content = jnp.concatenate([content] * 4, axis=0)
    mixed = sum(
        jnp.dot(part, content, preferred_element_type=jnp.float32) for part in parts_of(mixed, 3)
    )
    lane = lane_index((512, LANES))
    mixed = jnp.where(lane == 0, top, jnp.where(lane == 1, total, mixed))
    part_ref[...] = mixed.T[:PART_ROWS]


def refresh_kernel(part_ref, source_ref, msa_ref, sigmoid_ref, final_ref, out_ref):
    parts = [part_ref[k * PART_ROWS : k * PART_ROWS + 16, :] for k in range(16)]
    top = parts[0][0:1]
    for k in range(1, 16):
        top = jnp.maximum(top, parts[k][0:1])
    merged = jnp.zeros((16, 512), jnp.float32)
    for k in range(16):
        merged = merged + parts[k] * jnp.exp(parts[k][0:1] - top)
    mixed = merged[8:] / merged[1:2]
    shape = (LANES, 1024)
    spread = ones_where(row_index(shape) == lane_index(shape) // 8)
    keep = row_index((8, 1024)) == lane_index((8, 1024)) % 8
    gate_weight = block_diagonal(sigmoid_ref[...], 4)
    final_weight = block_diagonal(final_ref[...], 4)
    for q in range(4):
        stacked = jnp.concatenate(parts_of(mixed[:, q * LANES : (q + 1) * LANES], 3), axis=0)
        three = jnp.dot(stacked, spread, preferred_element_type=jnp.float32)
        wide = jnp.where(keep, three[:8] + three[8:16] + three[16:], 0.0)
        wide = jnp.sum(wide, 0, keepdims=True)
        wide = jnp.concatenate(
            [jnp.broadcast_to(wide[:, e * 256 : (e + 1) * 256], (HALF, 256)) for e in range(4)],
            axis=0,
        )
        gate = jax.nn.sigmoid(
            jnp.dot(
                source_ref[q * 256 : (q + 1) * 256, :],
                gate_weight,
                preferred_element_type=jnp.float32,
            )
        )
        change = jnp.dot(
            (gate * wide).astype(jnp.bfloat16), final_weight, preferred_element_type=jnp.float32
        )
        for e in range(4):
            lanes = slice((4 * q + e) * 256, (4 * q + e + 1) * 256)
            out_ref[:, lanes] = (
                msa_ref[:, lanes].astype(jnp.float32) + change[e * HALF : (e + 1) * HALF]
            ).astype(jnp.bfloat16)


def lane_index(shape):
    return lax.broadcasted_iota(jnp.int32, shape, len(shape) - 1)


def prepare_kernel(couple_ref, same_ref, table_ref, base_ref):
    step = pl.program_id(0)
    for p in range(4):
        here = pl.ds(step * 4 + p, 1)
        base_ref[p] = couple_ref[:, p].reshape(LANES, LANES).T + jnp.where(
            same_ref[here, :] > 0, table_ref[:, 1:2], table_ref[:, 0:1]
        )


def pair_kernel(
    left_a_ref,
    left_b_ref,
    left_mask_ref,
    right_ref,
    final_ref,
    base_ref,
    cover_ref,
    gain_ref,
    mapping_ref,
    mid_ref,
    source_ref,
    sent_ref,
    outer_ref,
    scale_ref,
    sides_ref,
):
    step = pl.program_id(0)
    steps = pl.num_programs(0)
    rows = 4
    low = lane_index((LANES, LANES)) < HALF
    odd = lax.axis_index("row") % 2
    col = lax.axis_index("col")

    def in_order(ref):
        blocks = []
        for block in range(16):
            turn = (block // 4 - col // 2 + 4) % 4
            place = jnp.where(turn == 2, 3, jnp.where(turn == 3, 1, jnp.where(turn == 1, 2, 0)))
            other = (block // 2 + col) % 2
            start = other * 512 + place * 128 + (block + odd) % 2 * 64
            blocks.append(ref[pl.ds(pl.multiple_of(start, HALF), HALF), :])
        return jnp.concatenate(blocks, axis=0)

    left = jnp.concatenate([in_order(left_a_ref), in_order(left_b_ref)], axis=1).T
    for n in range(8):
        outer_ref[:, n * 256 : (n + 1) * 256] = jnp.dot(
            left, right_ref[:, n * 256 : (n + 1) * 256], preferred_element_type=jnp.float32
        ).astype(jnp.bfloat16)

    @pl.when(step == 0)
    def _():
        both = lax.dot_general(
            in_order(left_mask_ref),
            right_ref[:, 2048:2176],
            (((0,), (0,)), ((), ())),
            preferred_element_type=jnp.float32,
        )
        both = 1.0 / jnp.maximum(both[:32], 1.0)
        scale_ref[...] = jnp.where(lane_index((16, LANES)) < HALF, both[:16], both[16:])

    gain = jnp.broadcast_to(gain_ref[...], (LANES, LANES))
    sources = []
    for p in range(rows):
        halves = []
        for top in (p * 32, 128 + p * 32):
            halves.append(
                jnp.concatenate(
                    [outer_ref[top : top + 32, d * LANES : (d + 1) * LANES] for d in range(16)],
                    axis=0,
                )
            )
        update = jnp.dot(
            final_ref[...],
            jnp.concatenate(halves, axis=1),
            preferred_element_type=jnp.float32,
        )
        a0, a1 = update[:LANES, :LANES], update[LANES:, :LANES]
        b0, b1 = update[:LANES, LANES:], update[LANES:, LANES:]
        update = jnp.where(low, a0, b1) + pltpu.roll(jnp.where(low, b0, a1), HALF, 1)
        mid = base_ref[p] + update * scale_ref[pl.ds(step * rows + p, 1), :]
        mid_ref[p] = mid
        mean = jnp.mean(mid, 0, keepdims=True)
        centred = mid - mean
        var = jnp.mean(centred * centred, 0, keepdims=True)
        source = (centred * lax.rsqrt(var + 1e-05) * gain).astype(jnp.bfloat16)
        source_ref[p] = source
        sources.append(source)
    sources = jnp.concatenate(sources, axis=1)
    for half in range(2):
        proj = jnp.dot(
            mapping_ref[half * 256 : (half + 1) * 256, :],
            sources,
            preferred_element_type=jnp.float32,
        )
        for p in range(rows):
            cover = cover_ref[pl.ds(step * rows + p, 1), :]
            gate = proj[:LANES, p * LANES : (p + 1) * LANES]
            value = proj[LANES:, p * LANES : (p + 1) * LANES]
            start = pl.multiple_of((half * 16 + step * rows + p) * LANES, LANES)
            sides_ref[pl.ds(start, LANES), :] = cover * jax.nn.sigmoid(gate) * value

    @pl.when(step == steps - 1)
    def _():
        def one(c, carry):
            sent_ref[c] = sides_ref[pl.ds(c, 32, stride=LANES), :].astype(jnp.bfloat16)
            return carry

        lax.fori_loop(0, LANES, one, 0, unroll=8)


def triangle_kernel(taken_ref, product_ref):
    low = lane_index((256, LANES)) < HALF
    sides = []
    for top in (0, 16):
        columns = []
        for q in range(4):
            even = taken_ref[:, 2 * q, top : top + 16, :].reshape(256, LANES).astype(jnp.float32)
            odd = taken_ref[:, 2 * q + 1, top : top + 16, :].reshape(256, LANES).astype(jnp.float32)
            first = jnp.where(low, even, pltpu.roll(odd, HALF, 1)).astype(jnp.bfloat16)
            second = jnp.where(low, pltpu.roll(even, HALF, 1), odd).astype(jnp.bfloat16)
            columns.append(
                jnp.concatenate(
                    [first.reshape(16, 1, 16, LANES), second.reshape(16, 1, 16, LANES)], axis=1
                ).reshape(512, LANES)
            )
        sides.append(jnp.concatenate(columns, axis=1))
    product = lax.dot_general(
        sides[0], sides[1], (((1,), (1,)), ((), ())), preferred_element_type=jnp.float32
    )
    product = product.reshape(16, 2, 16, 512)
    for q in range(4):
        first = product[:, 0, :, q * LANES : (q + 1) * LANES].reshape(256, LANES)
        second = product[:, 1, :, q * LANES : (q + 1) * LANES].reshape(256, LANES)
        product_ref[:, 2 * q] = (
            jnp.where(low, first, pltpu.roll(second, HALF, 1))
            .astype(jnp.bfloat16)
            .reshape(16, 16, LANES)
        )
        product_ref[:, 2 * q + 1] = (
            jnp.where(low, pltpu.roll(first, HALF, 1), second)
            .astype(jnp.bfloat16)
            .reshape(16, 16, LANES)
        )


def gate_kernel(source_ref, weight_ref, gate_ref):
    sources = jnp.concatenate([source_ref[p] for p in range(4)], axis=1)
    gate = jax.nn.sigmoid(
        jnp.dot(weight_ref[...], sources, preferred_element_type=jnp.float32)
    )
    for p in range(4):
        gate_ref[p] = gate[:, p * LANES : (p + 1) * LANES]


def finish_kernel(product_ref, mid_ref, gate_ref, final_ref, gain_ref, out_ref, normal_ref):
    step = pl.program_id(0)
    rows = 4

    @pl.when(step == 0)
    def _():
        total = product_ref[0].astype(jnp.float32)
        for c in range(1, LANES):
            total = total + product_ref[c].astype(jnp.float32)
        mean = total / LANES
        square = jnp.zeros_like(mean)
        for c in range(LANES):
            centred = product_ref[c].astype(jnp.float32) - mean
            square = square + centred * centred
        scale = lax.rsqrt(square / LANES + 1e-05)
        for c in range(LANES):
            normal_ref[c * 16 : (c + 1) * 16, :] = (
                product_ref[c].astype(jnp.float32) - mean
            ) * scale

    gain = jnp.broadcast_to(gain_ref[...], (LANES, LANES))
    centred = jnp.concatenate(
        [
            (normal_ref[pl.ds(step * rows + p, LANES, stride=16), :] * gain).astype(jnp.bfloat16)
            for p in range(rows)
        ],
        axis=1,
    )
    result = jnp.dot(final_ref[...], centred, preferred_element_type=jnp.float32)
    for p in range(rows):
        out = mid_ref[p] + gate_ref[p] * result[:, p * LANES : (p + 1) * LANES]
        out_ref[:, p] = out.T.reshape(2, HALF, LANES)


def whole(shape):
    return pl.BlockSpec(shape, lambda t: (0,) * len(shape), pipeline_mode=pl.Buffered(1))


def by_rows():
    return pl.BlockSpec((2, 4, HALF, LANES), lambda t: (0, t, 0, 0))


def by_pairs():
    return pl.BlockSpec((4, LANES, LANES), lambda t: (t, 0, 0))


PARAMS = pltpu.CompilerParams(
    vmem_limit_bytes=VMEM_LIMIT, dimension_semantics=("arbitrary",)
)


def cost(us):
    return pl.CostEstimate(flops=us * 10**9, bytes_accessed=us * 10**6, transcendentals=0)


def prepare_call(couple, same, table):
    return pl.pallas_call(
        prepare_kernel,
        grid=(4,),
        in_specs=[by_rows(), whole((16, LANES)), whole((LANES, 2))],
        out_specs=by_pairs(),
        out_shape=jax.ShapeDtypeStruct((16, LANES, LANES), jnp.float32),
        compiler_params=PARAMS,
        cost_estimate=cost(3),
        name="prepare",
    )(couple, same, table)


def pair_call(left, right, final, base, cover, gain, mapping):
    return pl.pallas_call(
        pair_kernel,
        grid=(4,),
        in_specs=[
            pl.BlockSpec((1024, LANES), lambda t: (0, t)),
            pl.BlockSpec((1024, LANES), lambda t: (0, t + 4)),
            pl.BlockSpec((1024, LANES), lambda t: (0, 8), pipeline_mode=pl.Buffered(1)),
            whole((1024, 2176)),
            whole((256, 512)),
            by_pairs(),
            whole((16, LANES)),
            whole((LANES, 1)),
            whole((512, LANES)),
        ],
        out_specs=[by_pairs(), by_pairs(), whole((LANES, 32, LANES))],
        out_shape=[
            jax.ShapeDtypeStruct((16, LANES, LANES), jnp.float32),
            jax.ShapeDtypeStruct((16, LANES, LANES), jnp.bfloat16),
            jax.ShapeDtypeStruct((LANES, 32, LANES), jnp.bfloat16),
        ],
        scratch_shapes=[
            pltpu.VMEM((256, 2048), jnp.bfloat16),
            pltpu.VMEM((16, LANES), jnp.float32),
            pltpu.VMEM((32 * LANES, LANES), jnp.float32),
        ],
        compiler_params=PARAMS,
        cost_estimate=cost(16),
        name="pair",
    )(left, left, left, right, final, base, cover, gain, mapping)


def triangle_call(taken):
    return pl.pallas_call(
        triangle_kernel,
        out_shape=jax.ShapeDtypeStruct((16, 8, 16, LANES), jnp.bfloat16),
        compiler_params=pltpu.CompilerParams(vmem_limit_bytes=VMEM_LIMIT),
        cost_estimate=cost(2),
        name="triangle",
    )(taken)


def gate_call(source, weight):
    return pl.pallas_call(
        gate_kernel,
        grid=(4,),
        in_specs=[by_pairs(), whole((LANES, LANES))],
        out_specs=by_pairs(),
        out_shape=jax.ShapeDtypeStruct((16, LANES, LANES), jnp.float32),
        compiler_params=PARAMS,
        cost_estimate=cost(2),
        name="gate",
    )(source, weight)


def finish_call(product, mid, gate, final, gain):
    return pl.pallas_call(
        finish_kernel,
        grid=(4,),
        in_specs=[
            whole((LANES, 16, LANES)),
            by_pairs(),
            by_pairs(),
            whole((LANES, LANES)),
            whole((LANES, 1)),
        ],
        out_specs=by_rows(),
        out_shape=jax.ShapeDtypeStruct((2, 16, HALF, LANES), jnp.float32),
        scratch_shapes=[pltpu.VMEM((LANES * 16, LANES), jnp.float32)],
        compiler_params=PARAMS,
        cost_estimate=cost(3),
        name="finish",
    )(product, mid, gate, final, gain)


def project_call(msa, cover, focus_gain, dyadic_gain, first, second):
    return pl.pallas_call(
        project_kernel,
        out_shape=[
            jax.ShapeDtypeStruct((2, 64, 1152), jnp.bfloat16),
            jax.ShapeDtypeStruct((64, 2176), jnp.bfloat16),
            jax.ShapeDtypeStruct((1024, 256), jnp.bfloat16),
            jax.ShapeDtypeStruct((16, 24, 256), jnp.float32),
        ],
        scratch_shapes=[pltpu.VMEM((2048, LANES), jnp.float32)],
        compiler_params=pltpu.CompilerParams(vmem_limit_bytes=ALL_VMEM),
        cost_estimate=cost(4),
        name="project",
    )(msa, cover, focus_gain, dyadic_gain, first, second)


def attend_call(source, cover, sums, asking, lookup, content):
    return pl.pallas_call(
        attend_kernel,
        out_shape=jax.ShapeDtypeStruct((PART_ROWS, 512), jnp.float32),
        compiler_params=pltpu.CompilerParams(vmem_limit_bytes=VMEM_LIMIT),
        cost_estimate=cost(3),
        name="attend",
    )(source, cover, sums, asking, lookup, content)


def refresh_call(parts, source, msa, gate, final):
    return pl.pallas_call(
        refresh_kernel,
        out_shape=jax.ShapeDtypeStruct((64, 4096), jnp.bfloat16),
        compiler_params=pltpu.CompilerParams(vmem_limit_bytes=VMEM_LIMIT),
        cost_estimate=cost(2),
        name="refresh",
    )(parts, source, msa, gate, final)


def ring_of_four(block, axis, step):
    half = block.shape[0] // 2
    back = lax.ppermute(block, axis, step(1))
    ahead = lax.ppermute(block, axis, step(-1))
    opposite = [
        lax.ppermute(back[:half], axis, step(1)),
        lax.ppermute(ahead[half:], axis, step(-1)),
    ]
    return jnp.concatenate([block, back, ahead] + opposite, axis=0)


def spread_left(left):
    n_row, n_col = lax.axis_size("row"), lax.axis_size("col")

    def route(flip):
        return [
            (r * n_col + c, (2 * c + (r + flip) % 2) * n_col + r // 2)
            for r in range(n_row)
            for c in range(n_col)
        ]

    def along(step):
        return [(c, (c + 2 * step) % n_col) for c in range(n_col)]

    both = jnp.concatenate(
        [lax.ppermute(left[flip], ("row", "col"), route(flip)) for flip in range(2)], axis=0
    )
    gathered = ring_of_four(both, "col", along)
    swapped = lax.ppermute(gathered, "col", [(c, c ^ 1) for c in range(n_col)])
    return jnp.concatenate([gathered, swapped], axis=0)


def halves_on_lanes(grid):
    return jnp.concatenate([grid[:16], grid[16:]], axis=1)


def local(
    alignment_tensor,
    supplement_align_cover,
    couple_tensor,
    couple_cover_grid,
    amino_strand_label,
    focus_scaling_vector,
    focus_asking_factor,
    focus_lookup_factor,
    focus_content_factor,
    focus_sigmoid_factor,
    focus_final_factor,
    dyadic_scaling_vector,
    dyadic_first_factor,
    dyadic_second_factor,
    dyadic_final_factor,
    strand_couple_table,
    trio_source_scaling,
    trio_mapping_factors,
    trio_sigmoid_factor,
    trio_middle_scaling,
    trio_final_factor,
):
    n_row = lax.axis_size("row")
    n_col = lax.axis_size("col")
    vertical_aminos = supplement_align_cover.shape[1]
    rows_res = couple_tensor.shape[0]
    width_o = dyadic_first_factor.shape[1]
    width_z = couple_tensor.shape[2]
    width_t = trio_final_factor.shape[0]
    left, right, source, sums = project_call(
        alignment_tensor,
        supplement_align_cover,
        focus_scaling_vector.reshape(1, HALF),
        dyadic_scaling_vector.reshape(1, HALF),
        dyadic_first_factor.T,
        dyadic_second_factor.T,
    )
    right_all = lax.all_gather(right, "row", axis=0, tiled=True)
    sums = lax.all_to_all(sums, "row", 0, 0, tiled=True)
    left, sums = lax.optimization_barrier((left, sums))
    parts = attend_call(
        source,
        supplement_align_cover,
        sums,
        focus_asking_factor,
        focus_lookup_factor.T,
        focus_content_factor.T,
    )
    left_rows, parts = lax.optimization_barrier((spread_left(left), parts))
    parts = lax.all_gather(parts, "row", axis=0, tiled=True)
    refreshed_supplement_align = refresh_call(
        parts, source, alignment_tensor, focus_sigmoid_factor, focus_final_factor
    )
    chain_rows = lax.dynamic_slice_in_dim(
        amino_strand_label, lax.axis_index("row") * rows_res, rows_res, 0
    )
    chain_cols = lax.dynamic_slice_in_dim(
        amino_strand_label, lax.axis_index("col") * vertical_aminos, vertical_aminos, 0
    )
    same = (chain_rows[:, None] == chain_cols[None, :]).astype(jnp.float32)
    final = (
        dyadic_final_factor.reshape(width_o, 16, 2, width_z)
        .transpose(2, 3, 1, 0)
        .reshape(2 * width_z, 16 * width_o)
    )
    base = prepare_call(
        couple_tensor.reshape(2, 16, vertical_aminos, width_z),
        halves_on_lanes(same),
        strand_couple_table.T,
    )
    pair_mid, tri_in, sides = pair_call(
        left_rows,
        right_all,
        final,
        base,
        halves_on_lanes(couple_cover_grid.astype(jnp.float32)),
        trio_source_scaling.reshape(width_z, 1),
        trio_mapping_factors.T,
    )
    taken = lax.all_to_all(sides, ("row", "col"), 0, 0, tiled=True)
    product = triangle_call(taken.reshape(n_row, n_col, 32, LANES))
    product = lax.all_to_all(
        product.reshape(n_row * n_col, 16, LANES), ("row", "col"), 0, 0, tiled=True
    )
    refreshed_couple_tensor = finish_call(
        product,
        pair_mid,
        gate_call(tri_in, trio_sigmoid_factor.T),
        trio_final_factor.T,
        trio_middle_scaling.reshape(width_t, 1),
    ).reshape(rows_res, vertical_aminos, width_z)
    return (refreshed_supplement_align, refreshed_couple_tensor)


def solution(mesh):
    in_specs = (
        P("row", "col"),
        P("row", "col"),
        P("row", "col", None),
        P("row", "col"),
        P(),
        P(),
        P(),
        P(),
        P(),
        P(),
        P(),
        P(),
        P(),
        P(),
        P(),
        P(),
        P(),
        P(),
        P(),
        P(),
        P(),
    )
    out_specs = (P("row", "col"), P("row", "col", None))
    return jax.shard_map(local, mesh=mesh, in_specs=in_specs, out_specs=out_specs, check_vma=False)
```

```python
import jax
import jax.numpy as jnp
from jax import lax
from jax.experimental import pallas as pl
from jax.experimental.pallas import tpu as pltpu
from jax.sharding import PartitionSpec as P

LANES = 128
HALF = 64
PART_ROWS = 40
VMEM_LIMIT = 50 * 1024 * 1024
ALL_VMEM = 64 * 1024 * 1024 - 8192


def row_index(shape):
    return lax.broadcasted_iota(jnp.int32, shape, 0)


def ones_where(keep):
    return jnp.where(keep, 1.0, 0.0).astype(jnp.bfloat16)


def repeat_lanes(w, times):
    b = w.shape[1]
    shape = (b, times * b)
    pick = ones_where(lane_index(shape) % b == row_index(shape))
    return jnp.dot(w, pick, preferred_element_type=jnp.float32).astype(jnp.bfloat16)


def block_diagonal(w, times):
    a, b = w.shape
    tall = jnp.concatenate([repeat_lanes(w, times)] * times, axis=0)
    keep = row_index(tall.shape) // a == lane_index(tall.shape) // b
    return jnp.where(keep, tall, jnp.zeros_like(tall))


def parts_of(x, count):
    out = []
    for _ in range(count):
        part = x.astype(jnp.bfloat16)
        out.append(part)
        x = x - part.astype(jnp.float32)
    return out


def project_kernel(
    msa_ref,
    cover_ref,
    focus_gain_ref,
    dyadic_gain_ref,
    first_ref,
    second_ref,
    left_ref,
    right_ref,
    source_ref,
    sums_ref,
    turn_ref,
):
    odd = lax.axis_index("row") % 2
    cover = cover_ref[...].astype(jnp.float32)
    cover_narrow = cover.astype(jnp.bfloat16)
    cover_turned = jnp.concatenate([cover, cover], axis=0).T
    square = (256, 256)
    average = jnp.where(
        row_index(square) // HALF == lane_index(square) // HALF, 1.0 / HALF, 0.0
    ).astype(jnp.bfloat16)
    first = block_diagonal(first_ref[...], 4)
    second = block_diagonal(second_ref[...], 4)
    focus_gain = jnp.concatenate([focus_gain_ref[...]] * 4, axis=1)
    dyadic_gain = jnp.concatenate([dyadic_gain_ref[...]] * 4, axis=1)
    for q in range(4):
        x = jnp.concatenate(
            [msa_ref[:, (4 * q + e) * 256 : (4 * q + e + 1) * 256] for e in range(4)], axis=0
        )
        mean = jnp.dot(x, average, preferred_element_type=jnp.float32)
        centred = x.astype(jnp.float32) - mean
        high, low = parts_of(centred * centred, 2)
        var = jnp.dot(high, average, preferred_element_type=jnp.float32) + jnp.dot(
            low, average, preferred_element_type=jnp.float32
        )
        normal = centred * lax.rsqrt(var + 1e-05)
        focus = (normal * focus_gain).astype(jnp.bfloat16)
        dyadic = (normal * dyadic_gain).astype(jnp.bfloat16)
        source_ref[q * 256 : (q + 1) * 256, :] = focus
        left = lax.dot_general(
            dyadic, first, (((1,), (1,)), ((), ())), preferred_element_type=jnp.float32
        )
        pick = ones_where(row_index((64, 512)) == 16 * q + lane_index((64, 512)) // 32)
        left_cover = jnp.dot(cover_narrow, pick, preferred_element_type=jnp.float32)
        right = lax.dot_general(
            second, dyadic, (((1,), (1,)), ((), ())), preferred_element_type=jnp.float32
        )
        pick = ones_where(row_index((64, 1024)) == 16 * q + lane_index((64, 1024)) // 64)
        focus_cover = jnp.dot(cover_narrow, pick, preferred_element_type=jnp.float32)
        for e in range(4):
            g = 4 * q + e
            rows = slice(e * HALF, (e + 1) * HALF)
            left_ref[(g // 8 + odd) % 2, :, (g % 8) * LANES : (g % 8 + 1) * LANES] = (
                left[rows] * left_cover[:, e * LANES : (e + 1) * LANES]
            ).astype(jnp.bfloat16)
            here = right[:, (e // 2) * LANES : (e // 2 + 1) * LANES]
            if e % 2:
                here = pltpu.roll(here, HALF, 1)
            for j in range(4):
                turn_ref[pl.ds(4 * g + j, 32, stride=HALF), :] = (
                    here[j * 32 : (j + 1) * 32] * cover_turned[4 * g + j : 4 * g + j + 1, :]
                )
            wide = focus_cover[:, e * 256 : (e + 1) * 256]
            total = jnp.sum(wide * focus[rows].astype(jnp.float32), 0, keepdims=True)
            for k in range(16):
                sums_ref[k, g : g + 1, :] = total[:, :LANES]
                sums_ref[k, 16 + g : 17 + g, :] = total[:, LANES:]
    count = jnp.sum(cover, 0, keepdims=True)
    for k in range(16):
        sums_ref[k, 32:, :] = jnp.zeros((8, LANES), jnp.float32)
        sums_ref[k, 32:33, :HALF] = count
    shape = (64, LANES)
    for h in range(2):
        pick = ones_where(
            (row_index(shape) == 32 * h + lane_index(shape)) & (lane_index(shape) < 32)
        )
        left_ref[(h + odd) % 2, :, 1024:1152] = jnp.dot(
            cover_narrow, pick, preferred_element_type=jnp.float32
        ).astype(jnp.bfloat16)
    pick = ones_where(row_index(shape) == lane_index(shape) % HALF)
    right_ref[:, 2048:2176] = jnp.dot(
        cover_narrow, pick, preferred_element_type=jnp.float32
    ).astype(jnp.bfloat16)
    for d in range(16):
        turned = turn_ref[d * LANES : (d + 1) * LANES, :].T
        right_ref[:, d * LANES : (d + 1) * LANES] = turned[:HALF].astype(jnp.bfloat16)


def attend_kernel(source_ref, cover_ref, sums_ref, asking_ref, lookup_ref, content_ref, part_ref):
    sums = sums_ref[0]
    for k in range(1, 16):
        sums = sums + sums_ref[k]
    count = jnp.broadcast_to(sums[32:33, :HALF], (16, HALF))
    shape = (16, HALF)
    count = jnp.where(lane_index(shape) // 4 == row_index(shape), count, 0.0)
    shape = (HALF, 256)
    pick = ones_where(row_index(shape) % 4 == lane_index(shape) // HALF)
    count = sum(
        jnp.dot(part, pick, preferred_element_type=jnp.float32) for part in parts_of(count, 2)
    )
    sums = jnp.concatenate([sums[:16], sums[16:32]], axis=1)
    query_mean = (sums / jnp.maximum(count, 1.0)).astype(jnp.bfloat16)
    query = (
        jnp.dot(query_mean, block_diagonal(asking_ref[...], 4), preferred_element_type=jnp.float32)
        * 8 ** (-0.5)
    )
    shape = (512, 256)
    spread = jnp.concatenate([jnp.broadcast_to(query[g : g + 1], (32, 256)) for g in range(16)], 0)
    spread = jnp.where(row_index(shape) % 32 == lane_index(shape) // 8, spread, 0.0)
    lookup = jnp.concatenate([lookup_ref[...].astype(jnp.float32)] * 8, axis=0)
    lookup = block_diagonal(lookup.astype(jnp.bfloat16), 4)
    ask = sum(
        jnp.dot(part, lookup, preferred_element_type=jnp.float32) for part in parts_of(spread, 3)
    )
    ask_parts = parts_of(ask, 3)
    logits = []
    for g in range(16):
        stacked = jnp.concatenate([part[g * 32 : (g + 1) * 32] for part in ask_parts], axis=0)
        three = lax.dot_general(
            stacked,
            source_ref[g * HALF : (g + 1) * HALF, :],
            (((1,), (1,)), ((), ())),
            preferred_element_type=jnp.float32,
        )
        logits.append(three[:32] + three[32:64] + three[64:])
    logits = jnp.concatenate(logits, axis=0)
    cover = cover_ref[...].astype(jnp.float32).T
    bias = jnp.where(cover > 0, 0.0, -1000000000.0)
    logits = logits + jnp.broadcast_to(bias[:, None, :], (64, 8, 64)).reshape(512, 64)
    top = jnp.max(logits, 1, keepdims=True)
    weights = jnp.exp(logits - top)
    total = jnp.sum(weights, 1, keepdims=True)
    weight_parts = parts_of(weights, 3)
    mixed = []
    for g in range(16):
        stacked = jnp.concatenate([part[g * 32 : (g + 1) * 32] for part in weight_parts], axis=0)
        three = jnp.dot(
            stacked, source_ref[g * HALF : (g + 1) * HALF, :], preferred_element_type=jnp.float32
        )
        mixed.append(three[:32] + three[32:64] + three[64:])
    mixed = jnp.concatenate(mixed, axis=0)
    mixed = jnp.where(row_index(shape) // 8 % 4 == lane_index(shape) // HALF, mixed, 0.0)
    small = (8, LANES)
    content = lax.dot_general(
        content_ref[...],
        ones_where(lane_index(small) == row_index(small) + 8),
        (((0,), (0,)), ((), ())),
        preferred_element_type=jnp.float32,
    ).astype(jnp.bfloat16)
    content = jnp.concatenate([content] * 4, axis=0)
    mixed = sum(
        jnp.dot(part, content, preferred_element_type=jnp.float32) for part in parts_of(mixed, 3)
    )
    lane = lane_index((512, LANES))
    mixed = jnp.where(lane == 0, top, jnp.where(lane == 1, total, mixed))
    part_ref[...] = mixed.T[:PART_ROWS]


def refresh_kernel(part_ref, source_ref, msa_ref, sigmoid_ref, final_ref, out_ref):
    parts = [part_ref[k * PART_ROWS : k * PART_ROWS + 16, :] for k in range(16)]
    top = parts[0][0:1]
    for k in range(1, 16):
        top = jnp.maximum(top, parts[k][0:1])
    merged = jnp.zeros((16, 512), jnp.float32)
    for k in range(16):
        merged = merged + parts[k] * jnp.exp(parts[k][0:1] - top)
    mixed = merged[8:] / merged[1:2]
    shape = (LANES, 1024)
    spread = ones_where(row_index(shape) == lane_index(shape) // 8)
    keep = row_index((8, 1024)) == lane_index((8, 1024)) % 8
    gate_weight = block_diagonal(sigmoid_ref[...], 4)
    final_weight = block_diagonal(final_ref[...], 4)
    for q in range(4):
        stacked = jnp.concatenate(parts_of(mixed[:, q * LANES : (q + 1) * LANES], 3), axis=0)
        three = jnp.dot(stacked, spread, preferred_element_type=jnp.float32)
        wide = jnp.where(keep, three[:8] + three[8:16] + three[16:], 0.0)
        wide = jnp.sum(wide, 0, keepdims=True)
        wide = jnp.concatenate(
            [jnp.broadcast_to(wide[:, e * 256 : (e + 1) * 256], (HALF, 256)) for e in range(4)],
            axis=0,
        )
        gate = jax.nn.sigmoid(
            jnp.dot(
                source_ref[q * 256 : (q + 1) * 256, :],
                gate_weight,
                preferred_element_type=jnp.float32,
            )
        )
        change = jnp.dot(
            (gate * wide).astype(jnp.bfloat16), final_weight, preferred_element_type=jnp.float32
        )
        for e in range(4):
            lanes = slice((4 * q + e) * 256, (4 * q + e + 1) * 256)
            out_ref[:, lanes] = (
                msa_ref[:, lanes].astype(jnp.float32) + change[e * HALF : (e + 1) * HALF]
            ).astype(jnp.bfloat16)


def lane_index(shape):
    return lax.broadcasted_iota(jnp.int32, shape, len(shape) - 1)


def prepare_kernel(couple_ref, same_ref, table_ref, base_ref):
    step = pl.program_id(0)
    for p in range(4):
        here = pl.ds(step * 4 + p, 1)
        base_ref[p] = couple_ref[:, p].reshape(LANES, LANES).T + jnp.where(
            same_ref[here, :] > 0, table_ref[:, 1:2], table_ref[:, 0:1]
        )


def pair_kernel(
    own_a_ref,
    own_b_ref,
    own_mask_ref,
    other_a_ref,
    other_b_ref,
    other_mask_ref,
    right_ref,
    final_ref,
    base_ref,
    cover_ref,
    gain_ref,
    mapping_ref,
    mid_ref,
    source_ref,
    sent_ref,
    outer_ref,
    scale_ref,
    sides_ref,
):
    step = pl.program_id(0)
    steps = pl.num_programs(0)
    rows = 4
    low = lane_index((LANES, LANES)) < HALF
    odd = lax.axis_index("row") % 2
    col = lax.axis_index("col")
    z = lax.axis_index("row") // 4

    def in_order(own_ref, other_ref):
        blocks = []
        for block in range(16):
            turned = z ^ (block // 4)
            holder = z ^ jnp.where(
                turned == 1, 2, jnp.where(turned == 2, 3, jnp.where(turned == 3, 1, 0))
            )
            turn = (holder - col // 2 + 4) % 4
            place = jnp.where(turn == 2, 3, jnp.where(turn == 3, 1, jnp.where(turn == 1, 2, 0)))
            start = pl.multiple_of(place * 128 + (block + odd) % 2 * 64, HALF)
            own = (block // 2 + col) % 2 == 0
            here = pl.ds(start, HALF)
            blocks.append(jnp.where(own, own_ref[here, :], other_ref[here, :]))
        return jnp.concatenate(blocks, axis=0)

    left = jnp.concatenate([in_order(own_a_ref, other_a_ref), in_order(own_b_ref, other_b_ref)], axis=1).T
    for n in range(8):
        outer_ref[:, n * 256 : (n + 1) * 256] = jnp.dot(
            left, right_ref[:, n * 256 : (n + 1) * 256], preferred_element_type=jnp.float32
        ).astype(jnp.bfloat16)

    @pl.when(step == 0)
    def _():
        both = lax.dot_general(
            in_order(own_mask_ref, other_mask_ref),
            right_ref[:, 2048:2176],
            (((0,), (0,)), ((), ())),
            preferred_element_type=jnp.float32,
        )
        both = 1.0 / jnp.maximum(both[:32], 1.0)
        scale_ref[...] = jnp.where(lane_index((16, LANES)) < HALF, both[:16], both[16:])

    gain = jnp.broadcast_to(gain_ref[...], (LANES, LANES))
    sources = []
    for p in range(rows):
        halves = []
        for top in (p * 32, 128 + p * 32):
            halves.append(
                jnp.concatenate(
                    [outer_ref[top : top + 32, d * LANES : (d + 1) * LANES] for d in range(16)],
                    axis=0,
                )
            )
        update = jnp.dot(
            final_ref[...],
            jnp.concatenate(halves, axis=1),
            preferred_element_type=jnp.float32,
        )
        a0, a1 = update[:LANES, :LANES], update[LANES:, :LANES]
        b0, b1 = update[:LANES, LANES:], update[LANES:, LANES:]
        update = jnp.where(low, a0, b1) + pltpu.roll(jnp.where(low, b0, a1), HALF, 1)
        mid = base_ref[p] + update * scale_ref[pl.ds(step * rows + p, 1), :]
        mid_ref[p] = mid
        mean = jnp.mean(mid, 0, keepdims=True)
        centred = mid - mean
        var = jnp.mean(centred * centred, 0, keepdims=True)
        source = (centred * lax.rsqrt(var + 1e-05) * gain).astype(jnp.bfloat16)
        source_ref[p] = source
        sources.append(source)
    sources = jnp.concatenate(sources, axis=1)
    for half in range(2):
        proj = jnp.dot(
            mapping_ref[half * 256 : (half + 1) * 256, :],
            sources,
            preferred_element_type=jnp.float32,
        )
        for p in range(rows):
            cover = cover_ref[pl.ds(step * rows + p, 1), :]
            gate = proj[:LANES, p * LANES : (p + 1) * LANES]
            value = proj[LANES:, p * LANES : (p + 1) * LANES]
            start = pl.multiple_of((half * 16 + step * rows + p) * LANES, LANES)
            sides_ref[pl.ds(start, LANES), :] = cover * jax.nn.sigmoid(gate) * value

    @pl.when(step == steps - 1)
    def _():
        def one(c, carry):
            sent_ref[c] = sides_ref[pl.ds(c, 32, stride=LANES), :].astype(jnp.bfloat16)
            return carry

        lax.fori_loop(0, LANES, one, 0, unroll=8)


def triangle_kernel(taken_ref, product_ref):
    low = lane_index((256, LANES)) < HALF
    sides = []
    for top in (0, 16):
        columns = []
        for q in range(4):
            even = taken_ref[:, 2 * q, top : top + 16, :].reshape(256, LANES).astype(jnp.float32)
            odd = taken_ref[:, 2 * q + 1, top : top + 16, :].reshape(256, LANES).astype(jnp.float32)
            first = jnp.where(low, even, pltpu.roll(odd, HALF, 1)).astype(jnp.bfloat16)
            second = jnp.where(low, pltpu.roll(even, HALF, 1), odd).astype(jnp.bfloat16)
            columns.append(
                jnp.concatenate(
                    [first.reshape(16, 1, 16, LANES), second.reshape(16, 1, 16, LANES)], axis=1
                ).reshape(512, LANES)
            )
        sides.append(jnp.concatenate(columns, axis=1))
    product = lax.dot_general(
        sides[0], sides[1], (((1,), (1,)), ((), ())), preferred_element_type=jnp.float32
    )
    product = product.reshape(16, 2, 16, 512)
    for q in range(4):
        first = product[:, 0, :, q * LANES : (q + 1) * LANES].reshape(256, LANES)
        second = product[:, 1, :, q * LANES : (q + 1) * LANES].reshape(256, LANES)
        product_ref[:, 2 * q] = (
            jnp.where(low, first, pltpu.roll(second, HALF, 1))
            .astype(jnp.bfloat16)
            .reshape(16, 16, LANES)
        )
        product_ref[:, 2 * q + 1] = (
            jnp.where(low, pltpu.roll(first, HALF, 1), second)
            .astype(jnp.bfloat16)
            .reshape(16, 16, LANES)
        )


def gate_kernel(source_ref, weight_ref, gate_ref):
    sources = jnp.concatenate([source_ref[p] for p in range(4)], axis=1)
    gate = jax.nn.sigmoid(
        jnp.dot(weight_ref[...], sources, preferred_element_type=jnp.float32)
    )
    for p in range(4):
        gate_ref[p] = gate[:, p * LANES : (p + 1) * LANES]


def finish_kernel(product_ref, mid_ref, gate_ref, final_ref, gain_ref, out_ref, normal_ref):
    step = pl.program_id(0)
    rows = 4

    @pl.when(step == 0)
    def _():
        total = product_ref[0].astype(jnp.float32)
        for c in range(1, LANES):
            total = total + product_ref[c].astype(jnp.float32)
        mean = total / LANES
        square = jnp.zeros_like(mean)
        for c in range(LANES):
            centred = product_ref[c].astype(jnp.float32) - mean
            square = square + centred * centred
        scale = lax.rsqrt(square / LANES + 1e-05)
        for c in range(LANES):
            normal_ref[c * 16 : (c + 1) * 16, :] = (
                product_ref[c].astype(jnp.float32) - mean
            ) * scale

    gain = jnp.broadcast_to(gain_ref[...], (LANES, LANES))
    centred = jnp.concatenate(
        [
            (normal_ref[pl.ds(step * rows + p, LANES, stride=16), :] * gain).astype(jnp.bfloat16)
            for p in range(rows)
        ],
        axis=1,
    )
    result = jnp.dot(final_ref[...], centred, preferred_element_type=jnp.float32)
    for p in range(rows):
        out = mid_ref[p] + gate_ref[p] * result[:, p * LANES : (p + 1) * LANES]
        out_ref[:, p] = out.T.reshape(2, HALF, LANES)


def whole(shape):
    return pl.BlockSpec(shape, lambda t: (0,) * len(shape), pipeline_mode=pl.Buffered(1))


def by_rows():
    return pl.BlockSpec((2, 4, HALF, LANES), lambda t: (0, t, 0, 0))


def by_pairs():
    return pl.BlockSpec((4, LANES, LANES), lambda t: (t, 0, 0))


PARAMS = pltpu.CompilerParams(
    vmem_limit_bytes=VMEM_LIMIT, dimension_semantics=("arbitrary",)
)


def cost(us):
    return pl.CostEstimate(flops=us * 10**9, bytes_accessed=us * 10**6, transcendentals=0)


def prepare_call(couple, same, table):
    return pl.pallas_call(
        prepare_kernel,
        grid=(4,),
        in_specs=[by_rows(), whole((16, LANES)), whole((LANES, 2))],
        out_specs=by_pairs(),
        out_shape=jax.ShapeDtypeStruct((16, LANES, LANES), jnp.float32),
        compiler_params=PARAMS,
        cost_estimate=cost(3),
        name="prepare",
    )(couple, same, table)


def by_left():
    return [
        pl.BlockSpec((512, LANES), lambda t: (0, t)),
        pl.BlockSpec((512, LANES), lambda t: (0, t + 4)),
        pl.BlockSpec((512, LANES), lambda t: (0, 8), pipeline_mode=pl.Buffered(1)),
    ]


def pair_call(own, other, right, final, base, cover, gain, mapping):
    return pl.pallas_call(
        pair_kernel,
        grid=(4,),
        in_specs=[
            *by_left(),
            *by_left(),
            whole((1024, 2176)),
            whole((256, 512)),
            by_pairs(),
            whole((16, LANES)),
            whole((LANES, 1)),
            whole((512, LANES)),
        ],
        out_specs=[by_pairs(), by_pairs(), whole((LANES, 32, LANES))],
        out_shape=[
            jax.ShapeDtypeStruct((16, LANES, LANES), jnp.float32),
            jax.ShapeDtypeStruct((16, LANES, LANES), jnp.bfloat16),
            jax.ShapeDtypeStruct((LANES, 32, LANES), jnp.bfloat16),
        ],
        scratch_shapes=[
            pltpu.VMEM((256, 2048), jnp.bfloat16),
            pltpu.VMEM((16, LANES), jnp.float32),
            pltpu.VMEM((32 * LANES, LANES), jnp.float32),
        ],
        compiler_params=PARAMS,
        cost_estimate=cost(16),
        name="pair",
    )(own, own, own, other, other, other, right, final, base, cover, gain, mapping)


def triangle_call(taken):
    return pl.pallas_call(
        triangle_kernel,
        out_shape=jax.ShapeDtypeStruct((16, 8, 16, LANES), jnp.bfloat16),
        compiler_params=pltpu.CompilerParams(vmem_limit_bytes=VMEM_LIMIT),
        cost_estimate=cost(2),
        name="triangle",
    )(taken)


def gate_call(source, weight):
    return pl.pallas_call(
        gate_kernel,
        grid=(4,),
        in_specs=[by_pairs(), whole((LANES, LANES))],
        out_specs=by_pairs(),
        out_shape=jax.ShapeDtypeStruct((16, LANES, LANES), jnp.float32),
        compiler_params=PARAMS,
        cost_estimate=cost(2),
        name="gate",
    )(source, weight)


def finish_call(product, mid, gate, final, gain):
    return pl.pallas_call(
        finish_kernel,
        grid=(4,),
        in_specs=[
            whole((LANES, 16, LANES)),
            by_pairs(),
            by_pairs(),
            whole((LANES, LANES)),
            whole((LANES, 1)),
        ],
        out_specs=by_rows(),
        out_shape=jax.ShapeDtypeStruct((2, 16, HALF, LANES), jnp.float32),
        scratch_shapes=[pltpu.VMEM((LANES * 16, LANES), jnp.float32)],
        compiler_params=PARAMS,
        cost_estimate=cost(3),
        name="finish",
    )(product, mid, gate, final, gain)


def project_call(msa, cover, focus_gain, dyadic_gain, first, second):
    return pl.pallas_call(
        project_kernel,
        out_shape=[
            jax.ShapeDtypeStruct((2, 64, 1152), jnp.bfloat16),
            jax.ShapeDtypeStruct((64, 2176), jnp.bfloat16),
            jax.ShapeDtypeStruct((1024, 256), jnp.bfloat16),
            jax.ShapeDtypeStruct((16, 40, LANES), jnp.float32),
        ],
        scratch_shapes=[pltpu.VMEM((2048, LANES), jnp.float32)],
        compiler_params=pltpu.CompilerParams(vmem_limit_bytes=ALL_VMEM),
        cost_estimate=cost(4),
        name="project",
    )(msa, cover, focus_gain, dyadic_gain, first, second)


def attend_call(source, cover, sums, asking, lookup, content):
    return pl.pallas_call(
        attend_kernel,
        out_shape=jax.ShapeDtypeStruct((PART_ROWS, 512), jnp.float32),
        compiler_params=pltpu.CompilerParams(vmem_limit_bytes=VMEM_LIMIT),
        cost_estimate=cost(3),
        name="attend",
    )(source, cover, sums, asking, lookup, content)


def refresh_call(parts, source, msa, gate, final):
    return pl.pallas_call(
        refresh_kernel,
        out_shape=jax.ShapeDtypeStruct((64, 4096), jnp.bfloat16),
        compiler_params=pltpu.CompilerParams(vmem_limit_bytes=VMEM_LIMIT),
        cost_estimate=cost(2),
        name="refresh",
    )(parts, source, msa, gate, final)


def ring_of_four(block, axis, step):
    half = block.shape[0] // 2
    back = lax.ppermute(block, axis, step(1))
    ahead = lax.ppermute(block, axis, step(-1))
    opposite = [
        lax.ppermute(back[:half], axis, step(1)),
        lax.ppermute(ahead[half:], axis, step(-1)),
    ]
    return jnp.concatenate([block, back, ahead] + opposite, axis=0)


def relay(origin, target):
    turned = origin ^ target
    return target ^ (0, 2, 3, 1)[turned]


def route_left(left):
    n_row, n_col = lax.axis_size("row"), lax.axis_size("col")

    def route(flip):
        return [
            (
                r * n_col + c,
                (2 * c + (r + flip) % 2) * n_col + 2 * relay(r // 4, c // 2) + r % 4 // 2,
            )
            for r in range(n_row)
            for c in range(n_col)
        ]

    return tuple(lax.ppermute(left[flip], ("row", "col"), route(flip)) for flip in range(2))


def spread_left(halves):
    n_col = lax.axis_size("col")

    def along(step):
        return [(c, (c + 2 * step) % n_col) for c in range(n_col)]

    gathered = ring_of_four(jnp.concatenate(halves, axis=0), "col", along)
    swapped = lax.ppermute(gathered, "col", [(c, c ^ 1) for c in range(n_col)])
    return gathered, swapped


def halves_on_lanes(grid):
    return jnp.concatenate([grid[:16], grid[16:]], axis=1)


def local(
    alignment_tensor,
    supplement_align_cover,
    couple_tensor,
    couple_cover_grid,
    amino_strand_label,
    focus_scaling_vector,
    focus_asking_factor,
    focus_lookup_factor,
    focus_content_factor,
    focus_sigmoid_factor,
    focus_final_factor,
    dyadic_scaling_vector,
    dyadic_first_factor,
    dyadic_second_factor,
    dyadic_final_factor,
    strand_couple_table,
    trio_source_scaling,
    trio_mapping_factors,
    trio_sigmoid_factor,
    trio_middle_scaling,
    trio_final_factor,
):
    n_row = lax.axis_size("row")
    n_col = lax.axis_size("col")
    vertical_aminos = supplement_align_cover.shape[1]
    rows_res = couple_tensor.shape[0]
    width_o = dyadic_first_factor.shape[1]
    width_z = couple_tensor.shape[2]
    width_t = trio_final_factor.shape[0]
    left, right, source, sums = project_call(
        alignment_tensor,
        supplement_align_cover,
        focus_scaling_vector.reshape(1, HALF),
        dyadic_scaling_vector.reshape(1, HALF),
        dyadic_first_factor.T,
        dyadic_second_factor.T,
    )
    right_all = lax.all_gather(right, "row", axis=0, tiled=True)
    left, sums = lax.optimization_barrier((route_left(left), sums))
    sums = lax.all_to_all(sums, "row", 0, 0, tiled=True)
    left, sums = lax.optimization_barrier((left, sums))
    parts = attend_call(
        source,
        supplement_align_cover,
        sums,
        focus_asking_factor,
        focus_lookup_factor.T,
        focus_content_factor.T,
    )
    left, parts = lax.optimization_barrier((left, parts))
    left_rows = spread_left(left)
    parts = lax.all_gather(parts, "row", axis=0, tiled=True)
    refreshed_supplement_align = refresh_call(
        parts, source, alignment_tensor, focus_sigmoid_factor, focus_final_factor
    )
    chain_rows = lax.dynamic_slice_in_dim(
        amino_strand_label, lax.axis_index("row") * rows_res, rows_res, 0
    )
    chain_cols = lax.dynamic_slice_in_dim(
        amino_strand_label, lax.axis_index("col") * vertical_aminos, vertical_aminos, 0
    )
    same = (chain_rows[:, None] == chain_cols[None, :]).astype(jnp.float32)
    final = (
        dyadic_final_factor.reshape(width_o, 16, 2, width_z)
        .transpose(2, 3, 1, 0)
        .reshape(2 * width_z, 16 * width_o)
    )
    base = prepare_call(
        couple_tensor.reshape(2, 16, vertical_aminos, width_z),
        halves_on_lanes(same),
        strand_couple_table.T,
    )
    pair_mid, tri_in, sides = pair_call(
        *left_rows,
        right_all,
        final,
        base,
        halves_on_lanes(couple_cover_grid.astype(jnp.float32)),
        trio_source_scaling.reshape(width_z, 1),
        trio_mapping_factors.T,
    )
    taken = lax.all_to_all(sides, ("row", "col"), 0, 0, tiled=True)
    product = triangle_call(taken.reshape(n_row, n_col, 32, LANES))
    product = lax.all_to_all(
        product.reshape(n_row * n_col, 16, LANES), ("row", "col"), 0, 0, tiled=True
    )
    refreshed_couple_tensor = finish_call(
        product,
        pair_mid,
        gate_call(tri_in, trio_sigmoid_factor.T),
        trio_final_factor.T,
        trio_middle_scaling.reshape(width_t, 1),
    ).reshape(rows_res, vertical_aminos, width_z)
    return (refreshed_supplement_align, refreshed_couple_tensor)


def solution(mesh):
    in_specs = (
        P("row", "col"),
        P("row", "col"),
        P("row", "col", None),
        P("row", "col"),
        P(),
        P(),
        P(),
        P(),
        P(),
        P(),
        P(),
        P(),
        P(),
        P(),
        P(),
        P(),
        P(),
        P(),
        P(),
        P(),
        P(),
    )
    out_specs = (P("row", "col"), P("row", "col", None))
    return jax.shard_map(local, mesh=mesh, in_specs=in_specs, out_specs=out_specs, check_vma=False)
```

```python
import jax
import jax.numpy as jnp
from jax import lax
from jax.experimental import pallas as pl
from jax.experimental.pallas import tpu as pltpu
from jax.sharding import PartitionSpec as P

LANES = 128
HALF = 64
PART_ROWS = 40
VMEM_LIMIT = 50 * 1024 * 1024
ALL_VMEM = 64 * 1024 * 1024 - 8192


def row_index(shape):
    return lax.broadcasted_iota(jnp.int32, shape, 0)


def ones_where(keep):
    return jnp.where(keep, 1.0, 0.0).astype(jnp.bfloat16)


def repeat_lanes(w, times):
    b = w.shape[1]
    shape = (b, times * b)
    pick = ones_where(lane_index(shape) % b == row_index(shape))
    return jnp.dot(w, pick, preferred_element_type=jnp.float32).astype(jnp.bfloat16)


def block_diagonal(w, times):
    a, b = w.shape
    tall = jnp.concatenate([repeat_lanes(w, times)] * times, axis=0)
    keep = row_index(tall.shape) // a == lane_index(tall.shape) // b
    return jnp.where(keep, tall, jnp.zeros_like(tall))


def parts_of(x, count):
    out = []
    for _ in range(count):
        part = x.astype(jnp.bfloat16)
        out.append(part)
        x = x - part.astype(jnp.float32)
    return out


def project_kernel(
    msa_ref,
    cover_ref,
    focus_gain_ref,
    dyadic_gain_ref,
    first_ref,
    second_ref,
    left_ref,
    right_ref,
    source_ref,
    sums_ref,
    turn_ref,
):
    odd = lax.axis_index("row") % 2
    cover = cover_ref[...].astype(jnp.float32)
    cover_narrow = cover.astype(jnp.bfloat16)
    cover_turned = jnp.concatenate([cover, cover], axis=0).T
    square = (256, 256)
    average = jnp.where(
        row_index(square) // HALF == lane_index(square) // HALF, 1.0 / HALF, 0.0
    ).astype(jnp.bfloat16)
    first = block_diagonal(first_ref[...], 4)
    second = block_diagonal(second_ref[...], 4)
    focus_gain = jnp.concatenate([focus_gain_ref[...]] * 4, axis=1)
    dyadic_gain = jnp.concatenate([dyadic_gain_ref[...]] * 4, axis=1)
    for q in range(4):
        x = jnp.concatenate(
            [msa_ref[:, (4 * q + e) * 256 : (4 * q + e + 1) * 256] for e in range(4)], axis=0
        )
        mean = jnp.dot(x, average, preferred_element_type=jnp.float32)
        centred = x.astype(jnp.float32) - mean
        high, low = parts_of(centred * centred, 2)
        var = jnp.dot(high, average, preferred_element_type=jnp.float32) + jnp.dot(
            low, average, preferred_element_type=jnp.float32
        )
        normal = centred * lax.rsqrt(var + 1e-05)
        focus = (normal * focus_gain).astype(jnp.bfloat16)
        dyadic = (normal * dyadic_gain).astype(jnp.bfloat16)
        source_ref[q * 256 : (q + 1) * 256, :] = focus
        left = lax.dot_general(
            dyadic, first, (((1,), (1,)), ((), ())), preferred_element_type=jnp.float32
        )
        pick = ones_where(row_index((64, 512)) == 16 * q + lane_index((64, 512)) // 32)
        left_cover = jnp.dot(cover_narrow, pick, preferred_element_type=jnp.float32)
        right = lax.dot_general(
            second, dyadic, (((1,), (1,)), ((), ())), preferred_element_type=jnp.float32
        )
        pick = ones_where(row_index((64, 1024)) == 16 * q + lane_index((64, 1024)) // 64)
        focus_cover = jnp.dot(cover_narrow, pick, preferred_element_type=jnp.float32)
        for e in range(4):
            g = 4 * q + e
            rows = slice(e * HALF, (e + 1) * HALF)
            left_ref[(g // 8 + odd) % 2, :, (g % 8) * LANES : (g % 8 + 1) * LANES] = (
                left[rows] * left_cover[:, e * LANES : (e + 1) * LANES]
            ).astype(jnp.bfloat16)
            here = right[:, (e // 2) * LANES : (e // 2 + 1) * LANES]
            if e % 2:
                here = pltpu.roll(here, HALF, 1)
            for j in range(4):
                turn_ref[pl.ds(4 * g + j, 32, stride=HALF), :] = (
                    here[j * 32 : (j + 1) * 32] * cover_turned[4 * g + j : 4 * g + j + 1, :]
                )
            wide = focus_cover[:, e * 256 : (e + 1) * 256]
            total = jnp.sum(wide * focus[rows].astype(jnp.float32), 0, keepdims=True)
            for k in range(16):
                sums_ref[k, g : g + 1, :] = total[:, :LANES]
                sums_ref[k, 16 + g : 17 + g, :] = total[:, LANES:]
    count = jnp.sum(cover, 0, keepdims=True)
    for k in range(16):
        sums_ref[k, 32:, :] = jnp.zeros((8, LANES), jnp.float32)
        sums_ref[k, 32:33, :HALF] = count
    shape = (64, LANES)
    for h in range(2):
        pick = ones_where(
            (row_index(shape) == 32 * h + lane_index(shape)) & (lane_index(shape) < 32)
        )
        left_ref[(h + odd) % 2, :, 1024:1152] = jnp.dot(
            cover_narrow, pick, preferred_element_type=jnp.float32
        ).astype(jnp.bfloat16)
    pick = ones_where(row_index(shape) == lane_index(shape) % HALF)
    right_ref[:, 2048:2176] = jnp.dot(
        cover_narrow, pick, preferred_element_type=jnp.float32
    ).astype(jnp.bfloat16)
    for d in range(16):
        turned = turn_ref[d * LANES : (d + 1) * LANES, :].T
        right_ref[:, d * LANES : (d + 1) * LANES] = turned[:HALF].astype(jnp.bfloat16)


def attend_kernel(source_ref, cover_ref, sums_ref, asking_ref, lookup_ref, content_ref, part_ref):
    sums = sums_ref[0]
    for k in range(1, 16):
        sums = sums + sums_ref[k]
    count = jnp.broadcast_to(sums[32:33, :HALF], (16, HALF))
    shape = (16, HALF)
    count = jnp.where(lane_index(shape) // 4 == row_index(shape), count, 0.0)
    shape = (HALF, 256)
    pick = ones_where(row_index(shape) % 4 == lane_index(shape) // HALF)
    count = sum(
        jnp.dot(part, pick, preferred_element_type=jnp.float32) for part in parts_of(count, 2)
    )
    sums = jnp.concatenate([sums[:16], sums[16:32]], axis=1)
    query_mean = (sums / jnp.maximum(count, 1.0)).astype(jnp.bfloat16)
    query = (
        jnp.dot(query_mean, block_diagonal(asking_ref[...], 4), preferred_element_type=jnp.float32)
        * 8 ** (-0.5)
    )
    shape = (512, 256)
    spread = jnp.concatenate([jnp.broadcast_to(query[g : g + 1], (32, 256)) for g in range(16)], 0)
    spread = jnp.where(row_index(shape) % 32 == lane_index(shape) // 8, spread, 0.0)
    lookup = jnp.concatenate([lookup_ref[...].astype(jnp.float32)] * 8, axis=0)
    lookup = block_diagonal(lookup.astype(jnp.bfloat16), 4)
    ask = sum(
        jnp.dot(part, lookup, preferred_element_type=jnp.float32) for part in parts_of(spread, 3)
    )
    ask_parts = parts_of(ask, 3)
    logits = []
    for g in range(16):
        stacked = jnp.concatenate([part[g * 32 : (g + 1) * 32] for part in ask_parts], axis=0)
        three = lax.dot_general(
            stacked,
            source_ref[g * HALF : (g + 1) * HALF, :],
            (((1,), (1,)), ((), ())),
            preferred_element_type=jnp.float32,
        )
        logits.append(three[:32] + three[32:64] + three[64:])
    logits = jnp.concatenate(logits, axis=0)
    cover = cover_ref[...].astype(jnp.float32).T
    bias = jnp.where(cover > 0, 0.0, -1000000000.0)
    logits = logits + jnp.broadcast_to(bias[:, None, :], (64, 8, 64)).reshape(512, 64)
    top = jnp.max(logits, 1, keepdims=True)
    weights = jnp.exp(logits - top)
    total = jnp.sum(weights, 1, keepdims=True)
    weight_parts = parts_of(weights, 3)
    mixed = []
    for g in range(16):
        stacked = jnp.concatenate([part[g * 32 : (g + 1) * 32] for part in weight_parts], axis=0)
        three = jnp.dot(
            stacked, source_ref[g * HALF : (g + 1) * HALF, :], preferred_element_type=jnp.float32
        )
        mixed.append(three[:32] + three[32:64] + three[64:])
    mixed = jnp.concatenate(mixed, axis=0)
    mixed = jnp.where(row_index(shape) // 8 % 4 == lane_index(shape) // HALF, mixed, 0.0)
    small = (8, LANES)
    content = lax.dot_general(
        content_ref[...],
        ones_where(lane_index(small) == row_index(small) + 8),
        (((0,), (0,)), ((), ())),
        preferred_element_type=jnp.float32,
    ).astype(jnp.bfloat16)
    content = jnp.concatenate([content] * 4, axis=0)
    mixed = sum(
        jnp.dot(part, content, preferred_element_type=jnp.float32) for part in parts_of(mixed, 3)
    )
    lane = lane_index((512, LANES))
    mixed = jnp.where(lane == 0, top, jnp.where(lane == 1, total, mixed))
    part_ref[...] = mixed.T[:PART_ROWS]


def refresh_kernel(part_ref, source_ref, msa_ref, sigmoid_ref, final_ref, out_ref):
    parts = [part_ref[k * PART_ROWS : k * PART_ROWS + 16, :] for k in range(16)]
    top = parts[0][0:1]
    for k in range(1, 16):
        top = jnp.maximum(top, parts[k][0:1])
    merged = jnp.zeros((16, 512), jnp.float32)
    for k in range(16):
        merged = merged + parts[k] * jnp.exp(parts[k][0:1] - top)
    mixed = merged[8:] / merged[1:2]
    shape = (LANES, 1024)
    spread = ones_where(row_index(shape) == lane_index(shape) // 8)
    keep = row_index((8, 1024)) == lane_index((8, 1024)) % 8
    gate_weight = block_diagonal(sigmoid_ref[...], 4)
    final_weight = block_diagonal(final_ref[...], 4)
    for q in range(4):
        stacked = jnp.concatenate(parts_of(mixed[:, q * LANES : (q + 1) * LANES], 3), axis=0)
        three = jnp.dot(stacked, spread, preferred_element_type=jnp.float32)
        wide = jnp.where(keep, three[:8] + three[8:16] + three[16:], 0.0)
        wide = jnp.sum(wide, 0, keepdims=True)
        wide = jnp.concatenate(
            [jnp.broadcast_to(wide[:, e * 256 : (e + 1) * 256], (HALF, 256)) for e in range(4)],
            axis=0,
        )
        gate = jax.nn.sigmoid(
            jnp.dot(
                source_ref[q * 256 : (q + 1) * 256, :],
                gate_weight,
                preferred_element_type=jnp.float32,
            )
        )
        change = jnp.dot(
            (gate * wide).astype(jnp.bfloat16), final_weight, preferred_element_type=jnp.float32
        )
        for e in range(4):
            lanes = slice((4 * q + e) * 256, (4 * q + e + 1) * 256)
            out_ref[:, lanes] = (
                msa_ref[:, lanes].astype(jnp.float32) + change[e * HALF : (e + 1) * HALF]
            ).astype(jnp.bfloat16)


def lane_index(shape):
    return lax.broadcasted_iota(jnp.int32, shape, len(shape) - 1)


def prepare_kernel(couple_ref, same_ref, table_ref, base_ref):
    step = pl.program_id(0)
    for p in range(4):
        here = pl.ds(step * 4 + p, 1)
        base_ref[p] = couple_ref[:, p].reshape(LANES, LANES).T + jnp.where(
            same_ref[here, :] > 0, table_ref[:, 1:2], table_ref[:, 0:1]
        )


def pair_kernel(
    own_a_ref,
    own_b_ref,
    own_mask_ref,
    other_a_ref,
    other_b_ref,
    other_mask_ref,
    right_ref,
    final_ref,
    base_ref,
    cover_ref,
    gain_ref,
    mapping_ref,
    mid_ref,
    source_ref,
    sent_ref,
    outer_ref,
    scale_ref,
    sides_ref,
):
    step = pl.program_id(0)
    steps = pl.num_programs(0)
    rows = 8
    low = lane_index((LANES, LANES)) < HALF
    odd = lax.axis_index("row") % 2
    col = lax.axis_index("col")
    z = lax.axis_index("row") // 4

    def in_order(own_ref, other_ref):
        blocks = []
        for block in range(16):
            turned = z ^ (block // 4)
            holder = z ^ jnp.where(
                turned == 1, 2, jnp.where(turned == 2, 3, jnp.where(turned == 3, 1, 0))
            )
            turn = (holder - col // 2 + 4) % 4
            place = jnp.where(turn == 2, 3, jnp.where(turn == 3, 1, jnp.where(turn == 1, 2, 0)))
            start = pl.multiple_of(place * 128 + (block + odd) % 2 * 64, HALF)
            own = (block // 2 + col) % 2 == 0
            here = pl.ds(start, HALF)
            blocks.append(jnp.where(own, own_ref[here, :], other_ref[here, :]))
        return jnp.concatenate(blocks, axis=0)

    left = jnp.concatenate([in_order(own_a_ref, other_a_ref), in_order(own_b_ref, other_b_ref)], axis=1).T
    for n in range(8):
        outer_ref[:, n * 256 : (n + 1) * 256] = jnp.dot(
            left, right_ref[:, n * 256 : (n + 1) * 256], preferred_element_type=jnp.float32
        ).astype(jnp.bfloat16)

    @pl.when(step == 0)
    def _():
        both = lax.dot_general(
            in_order(own_mask_ref, other_mask_ref),
            right_ref[:, 2048:2176],
            (((0,), (0,)), ((), ())),
            preferred_element_type=jnp.float32,
        )
        both = 1.0 / jnp.maximum(both[:32], 1.0)
        scale_ref[...] = jnp.where(lane_index((16, LANES)) < HALF, both[:16], both[16:])

    gain = jnp.broadcast_to(gain_ref[...], (LANES, LANES))
    sources = []
    for p in range(rows):
        halves = []
        for top in (p * 32, 256 + p * 32):
            halves.append(
                jnp.concatenate(
                    [outer_ref[top : top + 32, d * LANES : (d + 1) * LANES] for d in range(16)],
                    axis=0,
                )
            )
        update = jnp.dot(
            final_ref[...],
            jnp.concatenate(halves, axis=1),
            preferred_element_type=jnp.float32,
        )
        a0, a1 = update[:LANES, :LANES], update[LANES:, :LANES]
        b0, b1 = update[:LANES, LANES:], update[LANES:, LANES:]
        update = jnp.where(low, a0, b1) + pltpu.roll(jnp.where(low, b0, a1), HALF, 1)
        mid = base_ref[p] + update * scale_ref[pl.ds(step * rows + p, 1), :]
        mid_ref[p] = mid
        mean = jnp.mean(mid, 0, keepdims=True)
        centred = mid - mean
        var = jnp.mean(centred * centred, 0, keepdims=True)
        source = (centred * lax.rsqrt(var + 1e-05) * gain).astype(jnp.bfloat16)
        source_ref[p] = source
        sources.append(source)
    sources = jnp.concatenate(sources, axis=1)
    for half in range(2):
        proj = jnp.dot(
            mapping_ref[half * 256 : (half + 1) * 256, :],
            sources,
            preferred_element_type=jnp.float32,
        )
        for p in range(rows):
            cover = cover_ref[pl.ds(step * rows + p, 1), :]
            gate = proj[:LANES, p * LANES : (p + 1) * LANES]
            value = proj[LANES:, p * LANES : (p + 1) * LANES]
            start = pl.multiple_of((half * 16 + step * rows + p) * LANES, LANES)
            sides_ref[pl.ds(start, LANES), :] = cover * jax.nn.sigmoid(gate) * value

    @pl.when(step == steps - 1)
    def _():
        def one(c, carry):
            sent_ref[c] = sides_ref[pl.ds(c, 32, stride=LANES), :].astype(jnp.bfloat16)
            return carry

        lax.fori_loop(0, LANES, one, 0, unroll=8)


def triangle_kernel(taken_ref, product_ref):
    low = lane_index((256, LANES)) < HALF
    sides = []
    for top in (0, 16):
        columns = []
        for q in range(4):
            even = taken_ref[:, 2 * q, top : top + 16, :].reshape(256, LANES).astype(jnp.float32)
            odd = taken_ref[:, 2 * q + 1, top : top + 16, :].reshape(256, LANES).astype(jnp.float32)
            first = jnp.where(low, even, pltpu.roll(odd, HALF, 1)).astype(jnp.bfloat16)
            second = jnp.where(low, pltpu.roll(even, HALF, 1), odd).astype(jnp.bfloat16)
            columns.append(
                jnp.concatenate(
                    [first.reshape(16, 1, 16, LANES), second.reshape(16, 1, 16, LANES)], axis=1
                ).reshape(512, LANES)
            )
        sides.append(jnp.concatenate(columns, axis=1))
    product = lax.dot_general(
        sides[0], sides[1], (((1,), (1,)), ((), ())), preferred_element_type=jnp.float32
    )
    product = product.reshape(16, 2, 16, 512)
    for q in range(4):
        first = product[:, 0, :, q * LANES : (q + 1) * LANES].reshape(256, LANES)
        second = product[:, 1, :, q * LANES : (q + 1) * LANES].reshape(256, LANES)
        product_ref[:, 2 * q] = (
            jnp.where(low, first, pltpu.roll(second, HALF, 1))
            .astype(jnp.bfloat16)
            .reshape(16, 16, LANES)
        )
        product_ref[:, 2 * q + 1] = (
            jnp.where(low, pltpu.roll(first, HALF, 1), second)
            .astype(jnp.bfloat16)
            .reshape(16, 16, LANES)
        )


def gate_kernel(source_ref, weight_ref, gate_ref):
    sources = jnp.concatenate([source_ref[p] for p in range(4)], axis=1)
    gate = jax.nn.sigmoid(
        jnp.dot(weight_ref[...], sources, preferred_element_type=jnp.float32)
    )
    for p in range(4):
        gate_ref[p] = gate[:, p * LANES : (p + 1) * LANES]


def finish_kernel(product_ref, mid_ref, gate_ref, final_ref, gain_ref, out_ref, normal_ref):
    step = pl.program_id(0)
    rows = 8

    @pl.when(step == 0)
    def _():
        total = product_ref[0].astype(jnp.float32)
        for c in range(1, LANES):
            total = total + product_ref[c].astype(jnp.float32)
        mean = total / LANES
        square = jnp.zeros_like(mean)
        for c in range(LANES):
            centred = product_ref[c].astype(jnp.float32) - mean
            square = square + centred * centred
        scale = lax.rsqrt(square / LANES + 1e-05)
        for c in range(LANES):
            normal_ref[c * 16 : (c + 1) * 16, :] = (
                product_ref[c].astype(jnp.float32) - mean
            ) * scale

    gain = jnp.broadcast_to(gain_ref[...], (LANES, LANES))
    centred = jnp.concatenate(
        [
            (normal_ref[pl.ds(step * rows + p, LANES, stride=16), :] * gain).astype(jnp.bfloat16)
            for p in range(rows)
        ],
        axis=1,
    )
    result = jnp.dot(final_ref[...], centred, preferred_element_type=jnp.float32)
    for p in range(rows):
        out = mid_ref[p] + gate_ref[p] * result[:, p * LANES : (p + 1) * LANES]
        out_ref[:, p] = out.T.reshape(2, HALF, LANES)


def whole(shape):
    return pl.BlockSpec(shape, lambda t: (0,) * len(shape), pipeline_mode=pl.Buffered(1))


def by_rows(rows=4):
    return pl.BlockSpec((2, rows, HALF, LANES), lambda t: (0, t, 0, 0))


def by_pairs(rows=4):
    return pl.BlockSpec((rows, LANES, LANES), lambda t: (t, 0, 0))


PARAMS = pltpu.CompilerParams(
    vmem_limit_bytes=VMEM_LIMIT, dimension_semantics=("arbitrary",)
)


def cost(us):
    return pl.CostEstimate(flops=us * 10**9, bytes_accessed=us * 10**6, transcendentals=0)


def prepare_call(couple, same, table):
    return pl.pallas_call(
        prepare_kernel,
        grid=(4,),
        in_specs=[by_rows(), whole((16, LANES)), whole((LANES, 2))],
        out_specs=by_pairs(),
        out_shape=jax.ShapeDtypeStruct((16, LANES, LANES), jnp.float32),
        compiler_params=PARAMS,
        cost_estimate=cost(3),
        name="prepare",
    )(couple, same, table)


def by_left():
    return [
        pl.BlockSpec((512, 256), lambda t: (0, t)),
        pl.BlockSpec((512, 256), lambda t: (0, t + 2)),
        pl.BlockSpec((512, LANES), lambda t: (0, 8), pipeline_mode=pl.Buffered(1)),
    ]


def pair_call(own, other, right, final, base, cover, gain, mapping):
    return pl.pallas_call(
        pair_kernel,
        grid=(2,),
        in_specs=[
            *by_left(),
            *by_left(),
            whole((1024, 2176)),
            whole((256, 512)),
            by_pairs(8),
            whole((16, LANES)),
            whole((LANES, 1)),
            whole((512, LANES)),
        ],
        out_specs=[by_pairs(8), by_pairs(8), whole((LANES, 32, LANES))],
        out_shape=[
            jax.ShapeDtypeStruct((16, LANES, LANES), jnp.float32),
            jax.ShapeDtypeStruct((16, LANES, LANES), jnp.bfloat16),
            jax.ShapeDtypeStruct((LANES, 32, LANES), jnp.bfloat16),
        ],
        scratch_shapes=[
            pltpu.VMEM((512, 2048), jnp.bfloat16),
            pltpu.VMEM((16, LANES), jnp.float32),
            pltpu.VMEM((32 * LANES, LANES), jnp.float32),
        ],
        compiler_params=PARAMS,
        cost_estimate=cost(16),
        name="pair",
    )(own, own, own, other, other, other, right, final, base, cover, gain, mapping)


def triangle_call(taken):
    return pl.pallas_call(
        triangle_kernel,
        out_shape=jax.ShapeDtypeStruct((16, 8, 16, LANES), jnp.bfloat16),
        compiler_params=pltpu.CompilerParams(vmem_limit_bytes=VMEM_LIMIT),
        cost_estimate=cost(2),
        name="triangle",
    )(taken)


def gate_call(source, weight):
    return pl.pallas_call(
        gate_kernel,
        grid=(4,),
        in_specs=[by_pairs(), whole((LANES, LANES))],
        out_specs=by_pairs(),
        out_shape=jax.ShapeDtypeStruct((16, LANES, LANES), jnp.float32),
        compiler_params=PARAMS,
        cost_estimate=cost(2),
        name="gate",
    )(source, weight)


def finish_call(product, mid, gate, final, gain):
    return pl.pallas_call(
        finish_kernel,
        grid=(2,),
        in_specs=[
            whole((LANES, 16, LANES)),
            by_pairs(8),
            by_pairs(8),
            whole((LANES, LANES)),
            whole((LANES, 1)),
        ],
        out_specs=by_rows(8),
        out_shape=jax.ShapeDtypeStruct((2, 16, HALF, LANES), jnp.float32),
        scratch_shapes=[pltpu.VMEM((LANES * 16, LANES), jnp.float32)],
        compiler_params=PARAMS,
        cost_estimate=cost(3),
        name="finish",
    )(product, mid, gate, final, gain)


def project_call(msa, cover, focus_gain, dyadic_gain, first, second):
    return pl.pallas_call(
        project_kernel,
        out_shape=[
            jax.ShapeDtypeStruct((2, 64, 1152), jnp.bfloat16),
            jax.ShapeDtypeStruct((64, 2176), jnp.bfloat16),
            jax.ShapeDtypeStruct((1024, 256), jnp.bfloat16),
            jax.ShapeDtypeStruct((16, 40, LANES), jnp.float32),
        ],
        scratch_shapes=[pltpu.VMEM((2048, LANES), jnp.float32)],
        compiler_params=pltpu.CompilerParams(vmem_limit_bytes=ALL_VMEM),
        cost_estimate=cost(4),
        name="project",
    )(msa, cover, focus_gain, dyadic_gain, first, second)


def attend_call(source, cover, sums, asking, lookup, content):
    return pl.pallas_call(
        attend_kernel,
        out_shape=jax.ShapeDtypeStruct((PART_ROWS, 512), jnp.float32),
        compiler_params=pltpu.CompilerParams(vmem_limit_bytes=VMEM_LIMIT),
        cost_estimate=cost(3),
        name="attend",
    )(source, cover, sums, asking, lookup, content)


def refresh_call(parts, source, msa, gate, final):
    return pl.pallas_call(
        refresh_kernel,
        out_shape=jax.ShapeDtypeStruct((64, 4096), jnp.bfloat16),
        compiler_params=pltpu.CompilerParams(vmem_limit_bytes=VMEM_LIMIT),
        cost_estimate=cost(2),
        name="refresh",
    )(parts, source, msa, gate, final)


def ring_of_four(block, axis, step):
    half = block.shape[0] // 2
    back = lax.ppermute(block, axis, step(1))
    ahead = lax.ppermute(block, axis, step(-1))
    opposite = [
        lax.ppermute(back[:half], axis, step(1)),
        lax.ppermute(ahead[half:], axis, step(-1)),
    ]
    return jnp.concatenate([block, back, ahead] + opposite, axis=0)


def relay(origin, target):
    turned = origin ^ target
    return target ^ (0, 2, 3, 1)[turned]


def route_left(left):
    n_row, n_col = lax.axis_size("row"), lax.axis_size("col")

    def route(flip):
        return [
            (
                r * n_col + c,
                (2 * c + (r + flip) % 2) * n_col + 2 * relay(r // 4, c // 2) + r % 4 // 2,
            )
            for r in range(n_row)
            for c in range(n_col)
        ]

    return tuple(lax.ppermute(left[flip], ("row", "col"), route(flip)) for flip in range(2))


def spread_left(halves):
    n_col = lax.axis_size("col")

    def along(step):
        return [(c, (c + 2 * step) % n_col) for c in range(n_col)]

    gathered = ring_of_four(jnp.concatenate(halves, axis=0), "col", along)
    swapped = lax.ppermute(gathered, "col", [(c, c ^ 1) for c in range(n_col)])
    return gathered, swapped


def halves_on_lanes(grid):
    return jnp.concatenate([grid[:16], grid[16:]], axis=1)


def local(
    alignment_tensor,
    supplement_align_cover,
    couple_tensor,
    couple_cover_grid,
    amino_strand_label,
    focus_scaling_vector,
    focus_asking_factor,
    focus_lookup_factor,
    focus_content_factor,
    focus_sigmoid_factor,
    focus_final_factor,
    dyadic_scaling_vector,
    dyadic_first_factor,
    dyadic_second_factor,
    dyadic_final_factor,
    strand_couple_table,
    trio_source_scaling,
    trio_mapping_factors,
    trio_sigmoid_factor,
    trio_middle_scaling,
    trio_final_factor,
):
    n_row = lax.axis_size("row")
    n_col = lax.axis_size("col")
    vertical_aminos = supplement_align_cover.shape[1]
    rows_res = couple_tensor.shape[0]
    width_o = dyadic_first_factor.shape[1]
    width_z = couple_tensor.shape[2]
    width_t = trio_final_factor.shape[0]
    left, right, source, sums = project_call(
        alignment_tensor,
        supplement_align_cover,
        focus_scaling_vector.reshape(1, HALF),
        dyadic_scaling_vector.reshape(1, HALF),
        dyadic_first_factor.T,
        dyadic_second_factor.T,
    )
    right_all = lax.all_gather(right, "row", axis=0, tiled=True)
    left, sums = lax.optimization_barrier((route_left(left), sums))
    sums = lax.all_to_all(sums, "row", 0, 0, tiled=True)
    left, sums = lax.optimization_barrier((left, sums))
    parts = attend_call(
        source,
        supplement_align_cover,
        sums,
        focus_asking_factor,
        focus_lookup_factor.T,
        focus_content_factor.T,
    )
    left, parts = lax.optimization_barrier((left, parts))
    left_rows = spread_left(left)
    parts = lax.all_gather(parts, "row", axis=0, tiled=True)
    refreshed_supplement_align = refresh_call(
        parts, source, alignment_tensor, focus_sigmoid_factor, focus_final_factor
    )
    chain_rows = lax.dynamic_slice_in_dim(
        amino_strand_label, lax.axis_index("row") * rows_res, rows_res, 0
    )
    chain_cols = lax.dynamic_slice_in_dim(
        amino_strand_label, lax.axis_index("col") * vertical_aminos, vertical_aminos, 0
    )
    same = (chain_rows[:, None] == chain_cols[None, :]).astype(jnp.float32)
    final = (
        dyadic_final_factor.reshape(width_o, 16, 2, width_z)
        .transpose(2, 3, 1, 0)
        .reshape(2 * width_z, 16 * width_o)
    )
    base = prepare_call(
        couple_tensor.reshape(2, 16, vertical_aminos, width_z),
        halves_on_lanes(same),
        strand_couple_table.T,
    )
    pair_mid, tri_in, sides = pair_call(
        *left_rows,
        right_all,
        final,
        base,
        halves_on_lanes(couple_cover_grid.astype(jnp.float32)),
        trio_source_scaling.reshape(width_z, 1),
        trio_mapping_factors.T,
    )
    taken = lax.all_to_all(sides, ("row", "col"), 0, 0, tiled=True)
    product = triangle_call(taken.reshape(n_row, n_col, 32, LANES))
    product = lax.all_to_all(
        product.reshape(n_row * n_col, 16, LANES), ("row", "col"), 0, 0, tiled=True
    )
    refreshed_couple_tensor = finish_call(
        product,
        pair_mid,
        gate_call(tri_in, trio_sigmoid_factor.T),
        trio_final_factor.T,
        trio_middle_scaling.reshape(width_t, 1),
    ).reshape(rows_res, vertical_aminos, width_z)
    return (refreshed_supplement_align, refreshed_couple_tensor)


def solution(mesh):
    in_specs = (
        P("row", "col"),
        P("row", "col"),
        P("row", "col", None),
        P("row", "col"),
        P(),
        P(),
        P(),
        P(),
        P(),
        P(),
        P(),
        P(),
        P(),
        P(),
        P(),
        P(),
        P(),
        P(),
        P(),
        P(),
        P(),
    )
    out_specs = (P("row", "col"), P("row", "col", None))
    return jax.shard_map(local, mesh=mesh, in_specs=in_specs, out_specs=out_specs, check_vma=False)
```

```python
import jax
import jax.numpy as jnp
from jax import lax
from jax.experimental import pallas as pl
from jax.experimental.pallas import tpu as pltpu
from jax.sharding import PartitionSpec as P

LANES = 128
HALF = 64
PART_ROWS = 40
VMEM_LIMIT = 50 * 1024 * 1024
ALL_VMEM = 64 * 1024 * 1024 - 8192


def row_index(shape):
    return lax.broadcasted_iota(jnp.int32, shape, 0)


def ones_where(keep):
    return jnp.where(keep, 1.0, 0.0).astype(jnp.bfloat16)


def repeat_lanes(w, times):
    b = w.shape[1]
    shape = (b, times * b)
    pick = ones_where(lane_index(shape) % b == row_index(shape))
    return jnp.dot(w, pick, preferred_element_type=jnp.float32).astype(jnp.bfloat16)


def block_diagonal(w, times):
    a, b = w.shape
    tall = jnp.concatenate([repeat_lanes(w, times)] * times, axis=0)
    keep = row_index(tall.shape) // a == lane_index(tall.shape) // b
    return jnp.where(keep, tall, jnp.zeros_like(tall))


def parts_of(x, count):
    out = []
    for _ in range(count):
        part = x.astype(jnp.bfloat16)
        out.append(part)
        x = x - part.astype(jnp.float32)
    return out


def project_kernel(
    msa_ref,
    cover_ref,
    focus_gain_ref,
    dyadic_gain_ref,
    first_ref,
    second_ref,
    left_ref,
    right_ref,
    source_ref,
    sums_ref,
    turn_ref,
):
    odd = lax.axis_index("row") % 2
    cover = cover_ref[...].astype(jnp.float32)
    cover_narrow = cover.astype(jnp.bfloat16)
    cover_turned = jnp.concatenate([cover, cover], axis=0).T
    square = (256, 256)
    average = jnp.where(
        row_index(square) // HALF == lane_index(square) // HALF, 1.0 / HALF, 0.0
    ).astype(jnp.bfloat16)
    first = block_diagonal(first_ref[...], 4)
    second = block_diagonal(second_ref[...], 4)
    focus_gain = jnp.concatenate([focus_gain_ref[...]] * 4, axis=1)
    dyadic_gain = jnp.concatenate([dyadic_gain_ref[...]] * 4, axis=1)
    for q in range(4):
        x = jnp.concatenate(
            [msa_ref[:, (4 * q + e) * 256 : (4 * q + e + 1) * 256] for e in range(4)], axis=0
        )
        mean = jnp.dot(x, average, preferred_element_type=jnp.float32)
        centred = x.astype(jnp.float32) - mean
        high, low = parts_of(centred * centred, 2)
        var = jnp.dot(high, average, preferred_element_type=jnp.float32) + jnp.dot(
            low, average, preferred_element_type=jnp.float32
        )
        normal = centred * lax.rsqrt(var + 1e-05)
        focus = (normal * focus_gain).astype(jnp.bfloat16)
        dyadic = (normal * dyadic_gain).astype(jnp.bfloat16)
        source_ref[q * 256 : (q + 1) * 256, :] = focus
        left = lax.dot_general(
            dyadic, first, (((1,), (1,)), ((), ())), preferred_element_type=jnp.float32
        )
        pick = ones_where(row_index((64, 512)) == 16 * q + lane_index((64, 512)) // 32)
        left_cover = jnp.dot(cover_narrow, pick, preferred_element_type=jnp.float32)
        right = lax.dot_general(
            second, dyadic, (((1,), (1,)), ((), ())), preferred_element_type=jnp.float32
        )
        pick = ones_where(row_index((64, 1024)) == 16 * q + lane_index((64, 1024)) // 64)
        focus_cover = jnp.dot(cover_narrow, pick, preferred_element_type=jnp.float32)
        for e in range(4):
            g = 4 * q + e
            rows = slice(e * HALF, (e + 1) * HALF)
            left_ref[(g // 8 + odd) % 2, :, (g % 8) * LANES : (g % 8 + 1) * LANES] = (
                left[rows] * left_cover[:, e * LANES : (e + 1) * LANES]
            ).astype(jnp.bfloat16)
            here = right[:, (e // 2) * LANES : (e // 2 + 1) * LANES]
            if e % 2:
                here = pltpu.roll(here, HALF, 1)
            for j in range(4):
                turn_ref[pl.ds(4 * g + j, 32, stride=HALF), :] = (
                    here[j * 32 : (j + 1) * 32] * cover_turned[4 * g + j : 4 * g + j + 1, :]
                )
            wide = focus_cover[:, e * 256 : (e + 1) * 256]
            total = jnp.sum(wide * focus[rows].astype(jnp.float32), 0, keepdims=True)
            for k in range(4):
                sums_ref[k, g : g + 1, :] = total[:, :LANES]
                sums_ref[k, 16 + g : 17 + g, :] = total[:, LANES:]
    count = jnp.sum(cover, 0, keepdims=True)
    for k in range(4):
        sums_ref[k, 32:, :] = jnp.zeros((8, LANES), jnp.float32)
        sums_ref[k, 32:33, :HALF] = count
    shape = (64, LANES)
    for h in range(2):
        pick = ones_where(
            (row_index(shape) == 32 * h + lane_index(shape)) & (lane_index(shape) < 32)
        )
        left_ref[(h + odd) % 2, :, 1024:1152] = jnp.dot(
            cover_narrow, pick, preferred_element_type=jnp.float32
        ).astype(jnp.bfloat16)
    pick = ones_where(row_index(shape) == lane_index(shape) % HALF)
    right_ref[:, 2048:2176] = jnp.dot(
        cover_narrow, pick, preferred_element_type=jnp.float32
    ).astype(jnp.bfloat16)
    for d in range(16):
        turned = turn_ref[d * LANES : (d + 1) * LANES, :].T
        right_ref[:, d * LANES : (d + 1) * LANES] = turned[:HALF].astype(jnp.bfloat16)


def attend_kernel(source_ref, cover_ref, sums_ref, asking_ref, lookup_ref, content_ref, part_ref):
    sums = sums_ref[0]
    for k in range(1, 4):
        sums = sums + sums_ref[k]
    count = jnp.broadcast_to(sums[32:33, :HALF], (16, HALF))
    shape = (16, HALF)
    count = jnp.where(lane_index(shape) // 4 == row_index(shape), count, 0.0)
    shape = (HALF, 256)
    pick = ones_where(row_index(shape) % 4 == lane_index(shape) // HALF)
    count = sum(
        jnp.dot(part, pick, preferred_element_type=jnp.float32) for part in parts_of(count, 2)
    )
    sums = jnp.concatenate([sums[:16], sums[16:32]], axis=1)
    query_mean = (sums / jnp.maximum(count, 1.0)).astype(jnp.bfloat16)
    query = (
        jnp.dot(query_mean, block_diagonal(asking_ref[...], 4), preferred_element_type=jnp.float32)
        * 8 ** (-0.5)
    )
    shape = (512, 256)
    spread = jnp.concatenate([jnp.broadcast_to(query[g : g + 1], (32, 256)) for g in range(16)], 0)
    spread = jnp.where(row_index(shape) % 32 == lane_index(shape) // 8, spread, 0.0)
    lookup = jnp.concatenate([lookup_ref[...].astype(jnp.float32)] * 8, axis=0)
    lookup = block_diagonal(lookup.astype(jnp.bfloat16), 4)
    ask = sum(
        jnp.dot(part, lookup, preferred_element_type=jnp.float32) for part in parts_of(spread, 3)
    )
    ask_parts = parts_of(ask, 3)
    logits = []
    for g in range(16):
        stacked = jnp.concatenate([part[g * 32 : (g + 1) * 32] for part in ask_parts], axis=0)
        three = lax.dot_general(
            stacked,
            source_ref[g * HALF : (g + 1) * HALF, :],
            (((1,), (1,)), ((), ())),
            preferred_element_type=jnp.float32,
        )
        logits.append(three[:32] + three[32:64] + three[64:])
    logits = jnp.concatenate(logits, axis=0)
    cover = cover_ref[...].astype(jnp.float32).T
    bias = jnp.where(cover > 0, 0.0, -1000000000.0)
    logits = logits + jnp.broadcast_to(bias[:, None, :], (64, 8, 64)).reshape(512, 64)
    top = jnp.max(logits, 1, keepdims=True)
    weights = jnp.exp(logits - top)
    total = jnp.sum(weights, 1, keepdims=True)
    weight_parts = parts_of(weights, 3)
    mixed = []
    for g in range(16):
        stacked = jnp.concatenate([part[g * 32 : (g + 1) * 32] for part in weight_parts], axis=0)
        three = jnp.dot(
            stacked, source_ref[g * HALF : (g + 1) * HALF, :], preferred_element_type=jnp.float32
        )
        mixed.append(three[:32] + three[32:64] + three[64:])
    mixed = jnp.concatenate(mixed, axis=0)
    mixed = jnp.where(row_index(shape) // 8 % 4 == lane_index(shape) // HALF, mixed, 0.0)
    small = (8, LANES)
    content = lax.dot_general(
        content_ref[...],
        ones_where(lane_index(small) == row_index(small) + 8),
        (((0,), (0,)), ((), ())),
        preferred_element_type=jnp.float32,
    ).astype(jnp.bfloat16)
    content = jnp.concatenate([content] * 4, axis=0)
    mixed = sum(
        jnp.dot(part, content, preferred_element_type=jnp.float32) for part in parts_of(mixed, 3)
    )
    lane = lane_index((512, LANES))
    mixed = jnp.where(lane == 0, top, jnp.where(lane == 1, total, mixed))
    part_ref[...] = mixed.T[:PART_ROWS]


def refresh_kernel(part_ref, source_ref, msa_ref, sigmoid_ref, final_ref, out_ref):
    parts = [part_ref[k * PART_ROWS : k * PART_ROWS + 16, :] for k in range(16)]
    top = parts[0][0:1]
    for k in range(1, 16):
        top = jnp.maximum(top, parts[k][0:1])
    merged = jnp.zeros((16, 512), jnp.float32)
    for k in range(16):
        merged = merged + parts[k] * jnp.exp(parts[k][0:1] - top)
    mixed = merged[8:] / merged[1:2]
    shape = (LANES, 1024)
    spread = ones_where(row_index(shape) == lane_index(shape) // 8)
    keep = row_index((8, 1024)) == lane_index((8, 1024)) % 8
    gate_weight = block_diagonal(sigmoid_ref[...], 4)
    final_weight = block_diagonal(final_ref[...], 4)
    for q in range(4):
        stacked = jnp.concatenate(parts_of(mixed[:, q * LANES : (q + 1) * LANES], 3), axis=0)
        three = jnp.dot(stacked, spread, preferred_element_type=jnp.float32)
        wide = jnp.where(keep, three[:8] + three[8:16] + three[16:], 0.0)
        wide = jnp.sum(wide, 0, keepdims=True)
        wide = jnp.concatenate(
            [jnp.broadcast_to(wide[:, e * 256 : (e + 1) * 256], (HALF, 256)) for e in range(4)],
            axis=0,
        )
        gate = jax.nn.sigmoid(
            jnp.dot(
                source_ref[q * 256 : (q + 1) * 256, :],
                gate_weight,
                preferred_element_type=jnp.float32,
            )
        )
        change = jnp.dot(
            (gate * wide).astype(jnp.bfloat16), final_weight, preferred_element_type=jnp.float32
        )
        for e in range(4):
            lanes = slice((4 * q + e) * 256, (4 * q + e + 1) * 256)
            out_ref[:, lanes] = (
                msa_ref[:, lanes].astype(jnp.float32) + change[e * HALF : (e + 1) * HALF]
            ).astype(jnp.bfloat16)


def lane_index(shape):
    return lax.broadcasted_iota(jnp.int32, shape, len(shape) - 1)


def prepare_kernel(couple_ref, same_ref, table_ref, base_ref):
    step = pl.program_id(0)
    for p in range(4):
        here = pl.ds(step * 4 + p, 1)
        base_ref[p] = couple_ref[:, p].reshape(LANES, LANES).T + jnp.where(
            same_ref[here, :] > 0, table_ref[:, 1:2], table_ref[:, 0:1]
        )


def pair_kernel(
    own_a_ref,
    own_b_ref,
    own_mask_ref,
    other_a_ref,
    other_b_ref,
    other_mask_ref,
    right_ref,
    final_ref,
    base_ref,
    cover_ref,
    gain_ref,
    mapping_ref,
    mid_ref,
    source_ref,
    sent_ref,
    outer_ref,
    scale_ref,
    sides_ref,
):
    step = pl.program_id(0)
    steps = pl.num_programs(0)
    rows = 8
    low = lane_index((LANES, LANES)) < HALF
    odd = lax.axis_index("row") % 2
    col = lax.axis_index("col")
    z = lax.axis_index("row") // 4

    def in_order(own_ref, other_ref):
        blocks = []
        for block in range(16):
            turned = z ^ (block // 4)
            holder = z ^ jnp.where(
                turned == 1, 2, jnp.where(turned == 2, 3, jnp.where(turned == 3, 1, 0))
            )
            turn = (holder - col // 2 + 4) % 4
            place = jnp.where(turn == 2, 3, jnp.where(turn == 3, 1, jnp.where(turn == 1, 2, 0)))
            start = pl.multiple_of(place * 128 + (block + odd) % 2 * 64, HALF)
            own = (block // 2 + col) % 2 == 0
            here = pl.ds(start, HALF)
            blocks.append(jnp.where(own, own_ref[here, :], other_ref[here, :]))
        return jnp.concatenate(blocks, axis=0)

    left = jnp.concatenate([in_order(own_a_ref, other_a_ref), in_order(own_b_ref, other_b_ref)], axis=1).T
    for n in range(8):
        outer_ref[:, n * 256 : (n + 1) * 256] = jnp.dot(
            left, right_ref[:, n * 256 : (n + 1) * 256], preferred_element_type=jnp.float32
        ).astype(jnp.bfloat16)

    @pl.when(step == 0)
    def _():
        both = lax.dot_general(
            in_order(own_mask_ref, other_mask_ref),
            right_ref[:, 2048:2176],
            (((0,), (0,)), ((), ())),
            preferred_element_type=jnp.float32,
        )
        both = 1.0 / jnp.maximum(both[:32], 1.0)
        scale_ref[...] = jnp.where(lane_index((16, LANES)) < HALF, both[:16], both[16:])

    gain = jnp.broadcast_to(gain_ref[...], (LANES, LANES))
    sources = []
    for p in range(rows):
        halves = []
        for top in (p * 32, 256 + p * 32):
            halves.append(
                jnp.concatenate(
                    [outer_ref[top : top + 32, d * LANES : (d + 1) * LANES] for d in range(16)],
                    axis=0,
                )
            )
        update = jnp.dot(
            final_ref[...],
            jnp.concatenate(halves, axis=1),
            preferred_element_type=jnp.float32,
        )
        a0, a1 = update[:LANES, :LANES], update[LANES:, :LANES]
        b0, b1 = update[:LANES, LANES:], update[LANES:, LANES:]
        update = jnp.where(low, a0, b1) + pltpu.roll(jnp.where(low, b0, a1), HALF, 1)
        mid = base_ref[p] + update * scale_ref[pl.ds(step * rows + p, 1), :]
        mid_ref[p] = mid
        mean = jnp.mean(mid, 0, keepdims=True)
        centred = mid - mean
        var = jnp.mean(centred * centred, 0, keepdims=True)
        source = (centred * lax.rsqrt(var + 1e-05) * gain).astype(jnp.bfloat16)
        source_ref[p] = source
        sources.append(source)
    sources = jnp.concatenate(sources, axis=1)
    for half in range(2):
        proj = jnp.dot(
            mapping_ref[half * 256 : (half + 1) * 256, :],
            sources,
            preferred_element_type=jnp.float32,
        )
        for p in range(rows):
            cover = cover_ref[pl.ds(step * rows + p, 1), :]
            gate = proj[:LANES, p * LANES : (p + 1) * LANES]
            value = proj[LANES:, p * LANES : (p + 1) * LANES]
            start = pl.multiple_of((half * 16 + step * rows + p) * LANES, LANES)
            sides_ref[pl.ds(start, LANES), :] = cover * jax.nn.sigmoid(gate) * value

    @pl.when(step == steps - 1)
    def _():
        def one(c, carry):
            sent_ref[c] = sides_ref[pl.ds(c, 32, stride=LANES), :].astype(jnp.bfloat16)
            return carry

        lax.fori_loop(0, LANES, one, 0, unroll=8)


def triangle_kernel(taken_ref, product_ref):
    low = lane_index((256, LANES)) < HALF
    sides = []
    for top in (0, 16):
        columns = []
        for q in range(4):
            even = taken_ref[:, 2 * q, top : top + 16, :].reshape(256, LANES).astype(jnp.float32)
            odd = taken_ref[:, 2 * q + 1, top : top + 16, :].reshape(256, LANES).astype(jnp.float32)
            first = jnp.where(low, even, pltpu.roll(odd, HALF, 1)).astype(jnp.bfloat16)
            second = jnp.where(low, pltpu.roll(even, HALF, 1), odd).astype(jnp.bfloat16)
            columns.append(
                jnp.concatenate(
                    [first.reshape(16, 1, 16, LANES), second.reshape(16, 1, 16, LANES)], axis=1
                ).reshape(512, LANES)
            )
        sides.append(jnp.concatenate(columns, axis=1))
    product = lax.dot_general(
        sides[0], sides[1], (((1,), (1,)), ((), ())), preferred_element_type=jnp.float32
    )
    product = product.reshape(16, 2, 16, 512)
    for q in range(4):
        first = product[:, 0, :, q * LANES : (q + 1) * LANES].reshape(256, LANES)
        second = product[:, 1, :, q * LANES : (q + 1) * LANES].reshape(256, LANES)
        product_ref[:, 2 * q] = (
            jnp.where(low, first, pltpu.roll(second, HALF, 1))
            .astype(jnp.bfloat16)
            .reshape(16, 16, LANES)
        )
        product_ref[:, 2 * q + 1] = (
            jnp.where(low, pltpu.roll(first, HALF, 1), second)
            .astype(jnp.bfloat16)
            .reshape(16, 16, LANES)
        )


def gate_kernel(source_ref, weight_ref, gate_ref):
    sources = jnp.concatenate([source_ref[p] for p in range(4)], axis=1)
    gate = jax.nn.sigmoid(
        jnp.dot(weight_ref[...], sources, preferred_element_type=jnp.float32)
    )
    for p in range(4):
        gate_ref[p] = gate[:, p * LANES : (p + 1) * LANES]


def finish_kernel(product_ref, mid_ref, gate_ref, final_ref, gain_ref, out_ref, normal_ref):
    step = pl.program_id(0)
    rows = 8

    @pl.when(step == 0)
    def _():
        total = product_ref[0].astype(jnp.float32)
        for c in range(1, LANES):
            total = total + product_ref[c].astype(jnp.float32)
        mean = total / LANES
        square = jnp.zeros_like(mean)
        for c in range(LANES):
            centred = product_ref[c].astype(jnp.float32) - mean
            square = square + centred * centred
        scale = lax.rsqrt(square / LANES + 1e-05)
        for c in range(LANES):
            normal_ref[c * 16 : (c + 1) * 16, :] = (
                product_ref[c].astype(jnp.float32) - mean
            ) * scale

    gain = jnp.broadcast_to(gain_ref[...], (LANES, LANES))
    centred = jnp.concatenate(
        [
            (normal_ref[pl.ds(step * rows + p, LANES, stride=16), :] * gain).astype(jnp.bfloat16)
            for p in range(rows)
        ],
        axis=1,
    )
    result = jnp.dot(final_ref[...], centred, preferred_element_type=jnp.float32)
    for p in range(rows):
        out = mid_ref[p] + gate_ref[p] * result[:, p * LANES : (p + 1) * LANES]
        out_ref[:, p] = out.T.reshape(2, HALF, LANES)


def whole(shape):
    return pl.BlockSpec(shape, lambda t: (0,) * len(shape), pipeline_mode=pl.Buffered(1))


def by_rows(rows=4):
    return pl.BlockSpec((2, rows, HALF, LANES), lambda t: (0, t, 0, 0))


def by_pairs(rows=4):
    return pl.BlockSpec((rows, LANES, LANES), lambda t: (t, 0, 0))


PARAMS = pltpu.CompilerParams(
    vmem_limit_bytes=VMEM_LIMIT, dimension_semantics=("arbitrary",)
)


def cost(us):
    return pl.CostEstimate(flops=us * 10**9, bytes_accessed=us * 10**6, transcendentals=0)


def prepare_call(couple, same, table):
    return pl.pallas_call(
        prepare_kernel,
        grid=(4,),
        in_specs=[by_rows(), whole((16, LANES)), whole((LANES, 2))],
        out_specs=by_pairs(),
        out_shape=jax.ShapeDtypeStruct((16, LANES, LANES), jnp.float32),
        compiler_params=PARAMS,
        cost_estimate=cost(3),
        name="prepare",
    )(couple, same, table)


def by_left():
    return [
        pl.BlockSpec((512, 256), lambda t: (0, t)),
        pl.BlockSpec((512, 256), lambda t: (0, t + 2)),
        pl.BlockSpec((512, LANES), lambda t: (0, 8), pipeline_mode=pl.Buffered(1)),
    ]


def pair_call(own, other, right, final, base, cover, gain, mapping):
    return pl.pallas_call(
        pair_kernel,
        grid=(2,),
        in_specs=[
            *by_left(),
            *by_left(),
            whole((1024, 2176)),
            whole((256, 512)),
            by_pairs(8),
            whole((16, LANES)),
            whole((LANES, 1)),
            whole((512, LANES)),
        ],
        out_specs=[by_pairs(8), by_pairs(8), whole((LANES, 32, LANES))],
        out_shape=[
            jax.ShapeDtypeStruct((16, LANES, LANES), jnp.float32),
            jax.ShapeDtypeStruct((16, LANES, LANES), jnp.bfloat16),
            jax.ShapeDtypeStruct((LANES, 32, LANES), jnp.bfloat16),
        ],
        scratch_shapes=[
            pltpu.VMEM((512, 2048), jnp.bfloat16),
            pltpu.VMEM((16, LANES), jnp.float32),
            pltpu.VMEM((32 * LANES, LANES), jnp.float32),
        ],
        compiler_params=PARAMS,
        cost_estimate=cost(16),
        name="pair",
    )(own, own, own, other, other, other, right, final, base, cover, gain, mapping)


def triangle_call(taken):
    return pl.pallas_call(
        triangle_kernel,
        out_shape=jax.ShapeDtypeStruct((16, 8, 16, LANES), jnp.bfloat16),
        compiler_params=pltpu.CompilerParams(vmem_limit_bytes=VMEM_LIMIT),
        cost_estimate=cost(2),
        name="triangle",
    )(taken)


def gate_call(source, weight):
    return pl.pallas_call(
        gate_kernel,
        grid=(4,),
        in_specs=[by_pairs(), whole((LANES, LANES))],
        out_specs=by_pairs(),
        out_shape=jax.ShapeDtypeStruct((16, LANES, LANES), jnp.float32),
        compiler_params=PARAMS,
        cost_estimate=cost(2),
        name="gate",
    )(source, weight)


def finish_call(product, mid, gate, final, gain):
    return pl.pallas_call(
        finish_kernel,
        grid=(2,),
        in_specs=[
            whole((LANES, 16, LANES)),
            by_pairs(8),
            by_pairs(8),
            whole((LANES, LANES)),
            whole((LANES, 1)),
        ],
        out_specs=by_rows(8),
        out_shape=jax.ShapeDtypeStruct((2, 16, HALF, LANES), jnp.float32),
        scratch_shapes=[pltpu.VMEM((LANES * 16, LANES), jnp.float32)],
        compiler_params=PARAMS,
        cost_estimate=cost(3),
        name="finish",
    )(product, mid, gate, final, gain)


def project_call(msa, cover, focus_gain, dyadic_gain, first, second):
    return pl.pallas_call(
        project_kernel,
        out_shape=[
            jax.ShapeDtypeStruct((2, 64, 1152), jnp.bfloat16),
            jax.ShapeDtypeStruct((64, 2176), jnp.bfloat16),
            jax.ShapeDtypeStruct((1024, 256), jnp.bfloat16),
            jax.ShapeDtypeStruct((4, 40, LANES), jnp.float32),
        ],
        scratch_shapes=[pltpu.VMEM((2048, LANES), jnp.float32)],
        compiler_params=pltpu.CompilerParams(vmem_limit_bytes=ALL_VMEM),
        cost_estimate=cost(4),
        name="project",
    )(msa, cover, focus_gain, dyadic_gain, first, second)


def attend_call(source, cover, sums, asking, lookup, content):
    return pl.pallas_call(
        attend_kernel,
        out_shape=jax.ShapeDtypeStruct((PART_ROWS, 512), jnp.float32),
        compiler_params=pltpu.CompilerParams(vmem_limit_bytes=VMEM_LIMIT),
        cost_estimate=cost(3),
        name="attend",
    )(source, cover, sums, asking, lookup, content)


def refresh_call(parts, source, msa, gate, final):
    return pl.pallas_call(
        refresh_kernel,
        out_shape=jax.ShapeDtypeStruct((64, 4096), jnp.bfloat16),
        compiler_params=pltpu.CompilerParams(vmem_limit_bytes=VMEM_LIMIT),
        cost_estimate=cost(2),
        name="refresh",
    )(parts, source, msa, gate, final)


def ring_of_four(block, axis, step):
    half = block.shape[0] // 2
    back = lax.ppermute(block, axis, step(1))
    ahead = lax.ppermute(block, axis, step(-1))
    opposite = [
        lax.ppermute(back[:half], axis, step(1)),
        lax.ppermute(ahead[half:], axis, step(-1)),
    ]
    return jnp.concatenate([block, back, ahead] + opposite, axis=0)


def relay(origin, target):
    turned = origin ^ target
    return target ^ (0, 2, 3, 1)[turned]


def route_left(left):
    n_row, n_col = lax.axis_size("row"), lax.axis_size("col")

    def route(flip):
        return [
            (
                r * n_col + c,
                (2 * c + (r + flip) % 2) * n_col + 2 * relay(r // 4, c // 2) + r % 4 // 2,
            )
            for r in range(n_row)
            for c in range(n_col)
        ]

    return tuple(lax.ppermute(left[flip], ("row", "col"), route(flip)) for flip in range(2))


def spread_left(halves):
    n_col = lax.axis_size("col")

    def along(step):
        return [(c, (c + 2 * step) % n_col) for c in range(n_col)]

    gathered = ring_of_four(jnp.concatenate(halves, axis=0), "col", along)
    swapped = lax.ppermute(gathered, "col", [(c, c ^ 1) for c in range(n_col)])
    return gathered, swapped


def halves_on_lanes(grid):
    return jnp.concatenate([grid[:16], grid[16:]], axis=1)


def local(
    alignment_tensor,
    supplement_align_cover,
    couple_tensor,
    couple_cover_grid,
    amino_strand_label,
    focus_scaling_vector,
    focus_asking_factor,
    focus_lookup_factor,
    focus_content_factor,
    focus_sigmoid_factor,
    focus_final_factor,
    dyadic_scaling_vector,
    dyadic_first_factor,
    dyadic_second_factor,
    dyadic_final_factor,
    strand_couple_table,
    trio_source_scaling,
    trio_mapping_factors,
    trio_sigmoid_factor,
    trio_middle_scaling,
    trio_final_factor,
):
    n_row = lax.axis_size("row")
    n_col = lax.axis_size("col")
    vertical_aminos = supplement_align_cover.shape[1]
    rows_res = couple_tensor.shape[0]
    width_o = dyadic_first_factor.shape[1]
    width_z = couple_tensor.shape[2]
    width_t = trio_final_factor.shape[0]
    left, right, source, sums = project_call(
        alignment_tensor,
        supplement_align_cover,
        focus_scaling_vector.reshape(1, HALF),
        dyadic_scaling_vector.reshape(1, HALF),
        dyadic_first_factor.T,
        dyadic_second_factor.T,
    )
    right_all = lax.all_gather(right, "row", axis=0, tiled=True)
    left, sums = lax.optimization_barrier((route_left(left), sums))
    near = [[4 * z + x for x in range(4)] for z in range(4)]
    far = [[4 * z + x for z in range(4)] for x in range(4)]
    sums = lax.all_to_all(sums, "row", 0, 0, tiled=True, axis_index_groups=near)
    sums = jnp.broadcast_to(jnp.sum(sums, 0, keepdims=True), sums.shape)
    sums = lax.all_to_all(sums, "row", 0, 0, tiled=True, axis_index_groups=far)
    left, sums = lax.optimization_barrier((left, sums))
    parts = attend_call(
        source,
        supplement_align_cover,
        sums,
        focus_asking_factor,
        focus_lookup_factor.T,
        focus_content_factor.T,
    )
    left, parts = lax.optimization_barrier((left, parts))
    left_rows = spread_left(left)
    parts = lax.all_gather(parts, "row", axis=0, tiled=True)
    refreshed_supplement_align = refresh_call(
        parts, source, alignment_tensor, focus_sigmoid_factor, focus_final_factor
    )
    chain_rows = lax.dynamic_slice_in_dim(
        amino_strand_label, lax.axis_index("row") * rows_res, rows_res, 0
    )
    chain_cols = lax.dynamic_slice_in_dim(
        amino_strand_label, lax.axis_index("col") * vertical_aminos, vertical_aminos, 0
    )
    same = (chain_rows[:, None] == chain_cols[None, :]).astype(jnp.float32)
    final = (
        dyadic_final_factor.reshape(width_o, 16, 2, width_z)
        .transpose(2, 3, 1, 0)
        .reshape(2 * width_z, 16 * width_o)
    )
    base = prepare_call(
        couple_tensor.reshape(2, 16, vertical_aminos, width_z),
        halves_on_lanes(same),
        strand_couple_table.T,
    )
    pair_mid, tri_in, sides = pair_call(
        *left_rows,
        right_all,
        final,
        base,
        halves_on_lanes(couple_cover_grid.astype(jnp.float32)),
        trio_source_scaling.reshape(width_z, 1),
        trio_mapping_factors.T,
    )
    taken = lax.all_to_all(sides, ("row", "col"), 0, 0, tiled=True)
    product = triangle_call(taken.reshape(n_row, n_col, 32, LANES))
    product = lax.all_to_all(
        product.reshape(n_row * n_col, 16, LANES), ("row", "col"), 0, 0, tiled=True
    )
    refreshed_couple_tensor = finish_call(
        product,
        pair_mid,
        gate_call(tri_in, trio_sigmoid_factor.T),
        trio_final_factor.T,
        trio_middle_scaling.reshape(width_t, 1),
    ).reshape(rows_res, vertical_aminos, width_z)
    return (refreshed_supplement_align, refreshed_couple_tensor)


def solution(mesh):
    in_specs = (
        P("row", "col"),
        P("row", "col"),
        P("row", "col", None),
        P("row", "col"),
        P(),
        P(),
        P(),
        P(),
        P(),
        P(),
        P(),
        P(),
        P(),
        P(),
        P(),
        P(),
        P(),
        P(),
        P(),
        P(),
        P(),
    )
    out_specs = (P("row", "col"), P("row", "col", None))
    return jax.shard_map(local, mesh=mesh, in_specs=in_specs, out_specs=out_specs, check_vma=False)
```
